32 devices in a mesh: groups: 2 (over x), row: 8 (over z, y), col: 2 (over core).
Axes of the slice: x: 2, y: 2, z: 4, core: 2. Of those that a mesh axis runs over, the one named last changes fastest.
Arguments:
- users: bfloat16 [32768, 128], P(('groups', 'row', 'col')), parts along dimension 0, may hold values from -1.796875 to 1.796875
- items: bfloat16 [16384, 128], P(('groups', 'row', 'col')), parts along dimension 0, may hold values from -1.796875 to 1.796875
- ratings: bfloat16 [16, 2, 192, 128, 128], P(('groups', 'row'), 'col'), parts along dimension 0, may hold values from -6 to 6
- observed: int32 [16, 2, 192, 16, 128], P(('groups', 'row'), 'col'), parts along dimension 0, may hold values from 0 to 255
- tile_rows: int32 [16, 2, 192], P(('groups', 'row'), 'col'), parts along dimension 0, may hold values from 0 to 15
- tile_cols: int32 [16, 2, 192], P(('groups', 'row'), 'col'), parts along dimension 0, may hold values from 0 to 31
- tile_count: int32 [16, 2], P(('groups', 'row'), 'col'), parts along dimension 0, may hold values from 48 to 192, as said below
Outputs:
- users_new: bfloat16 [32768, 128], P(('groups', 'row', 'col')), parts along dimension 0
- items_new: bfloat16 [16384, 128], P(('groups', 'row', 'col')), parts along dimension 0
The draws below stay inside these ranges and needn't reach their ends.
There are 2 independent parts, one for each index of `groups`. The reference program is written for one: setup_inputs(seed, part) draws one part's arguments, and reference() takes and returns one part's arrays. A program takes and returns all parts, laid end to end along the dimension named above; each array names one. Nothing has to cross between parts.
Inputs may be any that keep to these rules, and one draw needn't show every extreme that they name: `tile_count`: slots at or after a device's count are ignored; some device's count is 192. `tile_rows`: user tile within the device's row block. `tile_cols`: item tile within the device's column block. `observed`: bit b of word w, column j: user 8 w + b of the tile rated item j.
All inputs are finite; a program needn't handle non-finite values.
Results may differ from the reference program's by a relative error of at most 0.014.
Values may be sent and summed in bfloat16 or wider, within the bound.
No kernel may reach another device: no remote copies, remote signals or barrier semaphores. Data moves between devices by JAX's collectives and lax.ppermute only.
A program may use at most 128 MiB of HBM per device.

```python
import jax
import jax.numpy as jnp
from jax import lax

RANK = 128
BLOCK = 128
UTILE = 16
ITILE = 32
TILES_DEV = 192
USERS = 16384
ITEMS = 8192
WORDS = 16
N_ROW = 8
N_COL = 2


def draw_tile_count(key, part):
    key = jax.random.fold_in(key, 7)
    key_counts, key_chosen = jax.random.split(key)
    counts = jax.random.randint(key_counts, (N_ROW, N_COL), max(1, TILES_DEV // 4), TILES_DEV + 1)
    chosen = jax.random.randint(key_chosen, (), 0, N_ROW * N_COL)
    places = jnp.arange(N_ROW * N_COL).reshape(N_ROW, N_COL)
    return jnp.where(places == chosen, TILES_DEV, counts).astype(jnp.int32)


def plant(result, stream_key, smallest, largest):
    longest = result.shape.index(max(result.shape))
    spots = []
    for shift in (0, 1):
        where = [jax.random.randint(jax.random.fold_in(stream_key, axis), (), 0, length) for axis, length in enumerate(result.shape)]
        where[longest] = (where[longest] + shift) % result.shape[longest]
        spots.append(tuple(where))
    return result.at[spots[0]].set(smallest).at[spots[1]].set(largest)


def block_scale(key, dims, cuts, smallest, top_value):
    level = 1.0
    for axis_at, parts in cuts:
        steps = jax.random.uniform(jax.random.fold_in(jax.random.fold_in(key, 6), axis_at), (parts,), jnp.float32, smallest / len(cuts), top_value / len(cuts))
        level = level * jnp.repeat(jnp.exp(steps), dims[axis_at] // parts).reshape((-1,) + (1,) * (len(dims) - 1 - axis_at))
    return level


def gaussian(own_key, dims, spread, reach, pieces=(), kind=jnp.bfloat16):
    drawn = jax.random.normal(own_key, dims, jnp.float32) * spread
    if len(pieces) > 0:
        drawn = block_scale(own_key, dims, pieces, -0.22, 0.18) * drawn
    return jnp.clip(drawn, min=-reach, max=reach).astype(kind)


def setup_inputs(seed: int = 0, part: int = 0) -> dict:
    seeds = jax.random.split(jax.random.key(seed), 8)
    part_keys = jax.random.split(jax.random.fold_in(seeds[7], part), 8)
    return {
        "users": gaussian(part_keys[0], (USERS, RANK), 0.3, 1.796875, ((0, 16),)),
        "items": gaussian(part_keys[1], (ITEMS, RANK), 0.3, 1.796875, ((0, 16),)),
        "ratings": gaussian(part_keys[2], (N_ROW, N_COL, TILES_DEV, BLOCK, BLOCK), 1.0, 6.0, ((0, 8), (1, 2))),
        "observed": plant(jax.random.randint(part_keys[3], (N_ROW, N_COL, TILES_DEV, WORDS, BLOCK), 0, 256), jax.random.fold_in(part_keys[3], 1), 0, 255).astype(jnp.int32),
        "tile_rows": plant(jax.random.randint(part_keys[4], (N_ROW, N_COL, TILES_DEV), 0, UTILE), jax.random.fold_in(part_keys[4], 1), 0, UTILE - 1).astype(jnp.int32),
        "tile_cols": plant(jax.random.randint(part_keys[5], (N_ROW, N_COL, TILES_DEV), 0, ITILE), jax.random.fold_in(part_keys[5], 1), 0, ITILE - 1).astype(jnp.int32),
        "tile_count": draw_tile_count(jax.random.fold_in(jax.random.fold_in(seeds[7], part), 71), part),
    }


def unpack_mask(words):
    offsets = jnp.arange(8, dtype=jnp.int32)
    planes = jnp.right_shift(words[..., :, None, :], offsets[:, None]) & 1
    target_shape = words.shape[:-2] + (words.shape[-2] * 8, words.shape[-1])
    return planes.reshape(target_shape)


def update_factor(factor, gradient, rate):
    values = factor.astype(jnp.float32)
    return (values - rate * (gradient + 0.05 * values)).astype(jnp.bfloat16)


def tile_residual(user_tiles, item_tiles, tiles, weights):
    predicted = jnp.einsum('tbk,tck->tbc', user_tiles.astype(jnp.float32), item_tiles.astype(jnp.float32))
    return (weights * (predicted - tiles.astype(jnp.float32))).astype(jnp.bfloat16)


def reference(users, items, ratings, observed, tile_rows, tile_cols, tile_count):
    rank = users.shape[-1]
    user_blocks = users.reshape(N_ROW, UTILE, BLOCK, rank)
    item_panels = items.reshape(N_ROW, N_COL, -1, rank).transpose(1, 0, 2, 3).reshape(N_COL, ITILE, BLOCK, rank)

    def tile_weights(row_index, col_index):
        live = jnp.arange(TILES_DEV, dtype=jnp.int32) < tile_count[row_index, col_index]
        bits_now = unpack_mask(observed[row_index, col_index])
        return jnp.where(live[:, None, None], bits_now, 0).astype(jnp.float32)

    def user_gradient(row_index):
        total = jnp.zeros((UTILE, BLOCK, rank), jnp.float32)
        for col_index in range(N_COL):
            user_tiles = user_blocks[row_index][tile_rows[row_index, col_index]]
            item_tiles = item_panels[col_index][tile_cols[row_index, col_index]]
            residual = tile_residual(user_tiles, item_tiles, ratings[row_index, col_index], tile_weights(row_index, col_index))
            grads = jnp.einsum('tbc,tck->tbk', residual.astype(jnp.float32), item_tiles.astype(jnp.float32))
            total = total + jax.ops.segment_sum(grads, tile_rows[row_index, col_index], num_segments=UTILE)
        return total

    user_grad = lax.map(user_gradient, jnp.arange(N_ROW, dtype=jnp.int32))
    fresh_blocks = update_factor(user_blocks, user_grad, 0.02)

    def item_step(carry, row_index):
        for col_index in range(N_COL):
            user_tiles = fresh_blocks[row_index][tile_rows[row_index, col_index]]
            item_tiles = item_panels[col_index][tile_cols[row_index, col_index]]
            residual = tile_residual(user_tiles, item_tiles, ratings[row_index, col_index], tile_weights(row_index, col_index))
            grads = jnp.einsum('tbc,tbk->tck', residual.astype(jnp.float32), user_tiles.astype(jnp.float32))
            carry = carry.at[col_index].add(jax.ops.segment_sum(grads, tile_cols[row_index, col_index], num_segments=ITILE))
        return carry, None

    item_grad, unused = lax.scan(item_step, jnp.zeros((N_COL, ITILE, BLOCK, rank), jnp.float32), jnp.arange(N_ROW, dtype=jnp.int32))
    item_grad = item_grad.reshape(N_COL, N_ROW, -1, rank).transpose(1, 0, 2, 3).reshape(items.shape)
    items_new = update_factor(items, item_grad, 0.005)
    users_new = fresh_blocks.reshape(users.shape)
    return users_new, items_new
```

```python
import functools

import jax
import jax.numpy as jnp
from jax import lax
from jax.experimental import pallas as pl
from jax.experimental.pallas import tpu as pltpu
from jax.sharding import PartitionSpec as P

BLOCK = 128
UNROLL = 4
VMEM_LIMIT = 48 * 1024 * 1024

NN = (((1,), (0,)), ((), ()))
NT = (((1,), (1,)), ((), ()))

vmem = functools.partial(pl.BlockSpec, memory_space=pltpu.VMEM)
smem = functools.partial(pl.BlockSpec, memory_space=pltpu.SMEM)
anywhere = functools.partial(pl.BlockSpec, memory_space=pl.ANY)


def params():
    return pltpu.CompilerParams(vmem_limit_bytes=VMEM_LIMIT)


def dot(a, b, dims):
    return lax.dot_general(a, b, dims, preferred_element_type=jnp.float32)


def rows_of(index):
    return pl.ds(pl.multiple_of(index * BLOCK, BLOCK), BLOCK)


def plan_kernel(
    slots, pad, shard_tiles, keys, info, rows, cols, ratings, observed,
    meta, tiles_out, words_out, place, sems,
):
    copy_tiles = pltpu.make_async_copy(ratings, tiles_out, sems.at[0])
    copy_words = pltpu.make_async_copy(observed, words_out, sems.at[1])
    copy_tiles.start()
    copy_words.start()
    count = info[0]
    me = info[1]

    def clear(k, _):
        place[k] = 0
        return _

    lax.fori_loop(0, keys + 1, clear, 0)

    def key_of(t):
        return jnp.bitwise_xor(cols[t] // shard_tiles, me) if keys > 1 else 0

    def tally(t, _):
        k = key_of(t)
        place[k + 1] = place[k + 1] + 1
        return _

    lax.fori_loop(0, count, tally, 0)

    def sums(k, total):
        total = total + place[k]
        place[k] = total
        meta[3 * pad + k] = total
        return total

    lax.fori_loop(0, keys + 1, sums, 0)

    def put(t, _):
        k = key_of(t)
        at = place[k]
        place[k] = at + 1
        meta[at] = t
        meta[pad + at] = rows[t]
        meta[2 * pad + at] = cols[t] % shard_tiles if keys > 1 else cols[t]
        return _

    lax.fori_loop(0, count, put, 0)

    def fill(at, _):
        meta[at] = 0
        meta[pad + at] = 0
        meta[2 * pad + at] = 0
        return _

    lax.fori_loop(count, pad, fill, 0)
    copy_tiles.wait()
    copy_words.wait()


def stage_loop(pad, key, meta, group):
    low = meta[3 * pad + key]
    high = meta[3 * pad + key + 1]

    def step(i, _):
        group([
            (meta[at], meta[pad + at], meta[2 * pad + at], at < high)
            for at in [low + i * UNROLL + j for j in range(UNROLL)]
        ])
        return _

    lax.fori_loop(0, (high - low + UNROLL - 1) // UNROLL, step, 0)


def masked_residual(predicted, tiles, words, slot, live):
    bit = jnp.left_shift(1, lax.broadcasted_iota(jnp.int32, (8, BLOCK), 0))
    bit = jnp.where(live, bit, 0)
    parts = []
    for w in range(BLOCK // 8):
        seen = jnp.broadcast_to(words[slot, pl.ds(w, 1), :], (8, BLOCK)) & bit
        gap = predicted[8 * w : 8 * w + 8] - tiles[slot, pl.ds(8 * w, 8), :].astype(jnp.float32)
        parts.append(jnp.where(seen != 0, gap, 0.0))
    return jnp.concatenate(parts, axis=0).astype(jnp.bfloat16)


def user_kernel(pad, key, last, meta, tiles, words, users, shard, *rest):
    if key:
        prior, total = rest[0], rest[1]
    else:
        total = rest[0]
        total[...] = jnp.zeros_like(total)
    flipped = rest[-1]
    for v in range(shard.shape[0] // BLOCK):
        flipped[v * BLOCK : (v + 1) * BLOCK] = shard[v * BLOCK : (v + 1) * BLOCK].T

    def group(entries):
        terms = []
        for slot, u, v, live in entries:
            predicted = dot(users[rows_of(u), :], flipped[rows_of(v), :], NN)
            residual = masked_residual(predicted, tiles, words, slot, live)
            terms.append(dot(residual, shard[rows_of(v), :], NN))
        for (slot, u, v, live), term in zip(entries, terms):
            total[rows_of(u), :] += term

    stage_loop(pad, key, meta, group)
    if last:
        rest[-2][...] = total[...].astype(jnp.bfloat16)


def fresh_kernel(mine, theirs, users, fresh, turned):
    for u in range(users.shape[0] // BLOCK):
        at = slice(u * BLOCK, (u + 1) * BLOCK)
        values = users[at].astype(jnp.float32)
        gradient = mine[at].astype(jnp.float32) + theirs[at].astype(jnp.float32)
        new = (values - 0.02 * (gradient + 0.05 * values)).astype(jnp.bfloat16)
        fresh[at] = new
        turned[at] = new.T


def item_kernel(pad, key, meta, tiles, words, fresh, turned, shard, out, total, flipped):
    total[...] = jnp.zeros_like(total)
    for v in range(shard.shape[0] // BLOCK):
        flipped[v * BLOCK : (v + 1) * BLOCK] = shard[v * BLOCK : (v + 1) * BLOCK].T

    def group(entries):
        terms = []
        for slot, u, v, live in entries:
            predicted = dot(fresh[rows_of(u), :], flipped[rows_of(v), :], NN)
            residual = masked_residual(predicted, tiles, words, slot, live)
            terms.append(dot(turned[rows_of(u), :], residual, NN))
        for (slot, u, v, live), term in zip(entries, terms):
            total[rows_of(v), :] += term

    stage_loop(pad, key, meta, group)
    for v in range(shard.shape[0] // BLOCK):
        at = slice(v * BLOCK, (v + 1) * BLOCK)
        out[at] = total[at].T.astype(out.dtype)


def body(n_row, n_col, users, items, ratings, observed, tile_rows, tile_cols, tile_count):
    tiles = ratings[0, 0]
    words = observed[0, 0]
    slots = tiles.shape[0]
    rank = users.shape[-1]
    pad = slots + 8
    shard_rows = items.shape[0]
    direct = shard_rows % BLOCK == 0 and n_row & (n_row - 1) == 0
    keys = n_row if direct else 1
    row_at = lax.axis_index("row")
    col_at = lax.axis_index("col")

    def swap_row(x, k):
        return lax.ppermute(x, "row", [(i, i ^ k) for i in range(n_row)])

    def swap_col(x):
        return lax.ppermute(x, "col", [(i, i ^ 1) for i in range(n_col)])

    peer_users = swap_col(users)
    if direct:
        shards = [items] + [swap_row(items, k) for k in range(1, n_row)]
    else:
        shards = [lax.all_gather(items, "row", axis=0, tiled=True)]
    wide = shards[0].shape[0]

    info = jnp.stack([tile_count[0, 0], row_at.astype(jnp.int32)])
    meta, tiles_in, words_in = pl.pallas_call(
        functools.partial(plan_kernel, slots, pad, wide // BLOCK, keys),
        out_shape=(
            jax.ShapeDtypeStruct((3 * pad + keys + 8,), jnp.int32),
            pltpu.VMEM(tiles.shape, tiles.dtype),
            pltpu.VMEM(words.shape, words.dtype),
        ),
        in_specs=[smem(), smem(), smem(), anywhere(), anywhere()],
        out_specs=(smem(), vmem(), vmem()),
        scratch_shapes=[pltpu.SMEM((keys + 1,), jnp.int32), pltpu.SemaphoreType.DMA((2,))],
        compiler_params=params(),
        name="plan",
    )(info, tile_rows[0, 0], tile_cols[0, 0], tiles, words)

    first = col_at == 0
    panel = jnp.concatenate(
        [jnp.where(first, users, peer_users), jnp.where(first, peer_users, users)], axis=0
    )
    cost = pl.CostEstimate(
        flops=4 * slots * BLOCK * BLOCK * rank // keys,
        bytes_accessed=(slots // keys) * BLOCK * BLOCK * 4,
        transcendentals=0,
    )
    total = None
    terms = None
    for key in range(keys):
        last = key == keys - 1
        shapes = [pltpu.VMEM(panel.shape, jnp.float32)]
        if last:
            shapes.append(jax.ShapeDtypeStruct(panel.shape, jnp.bfloat16))
        operands = [meta, tiles_in, words_in, panel, shards[key]] + ([total] if key else [])
        outs = pl.pallas_call(
            functools.partial(user_kernel, pad, key, last),
            out_shape=tuple(shapes),
            in_specs=[smem()] + [vmem()] * (len(operands) - 1),
            out_specs=tuple([vmem()] * len(shapes)),
            input_output_aliases={5: 0} if key else {},
            scratch_shapes=[pltpu.VMEM((wide, rank), jnp.bfloat16)],
            compiler_params=params(),
            cost_estimate=cost,
            name="user_terms",
        )(*operands)
        total = outs[0]
        terms = outs[-1]

    peer_terms = swap_col(terms)
    fresh, turned = pl.pallas_call(
        fresh_kernel,
        out_shape=(pltpu.VMEM(panel.shape, jnp.bfloat16), pltpu.VMEM(panel.shape, jnp.bfloat16)),
        in_specs=[vmem()] * 3,
        out_specs=(vmem(), vmem()),
        compiler_params=params(),
        name="fresh",
    )(terms, peer_terms, panel)
    users_new = lax.dynamic_slice_in_dim(fresh, col_at * users.shape[0], users.shape[0], 0)

    def item_terms(key, kind):
        return pl.pallas_call(
            functools.partial(item_kernel, pad, key),
            out_shape=jax.ShapeDtypeStruct((wide, rank), kind),
            in_specs=[smem()] + [vmem()] * 5,
            out_specs=vmem(),
            scratch_shapes=[
                pltpu.VMEM((wide, rank), jnp.float32),
                pltpu.VMEM((wide, rank), jnp.bfloat16),
            ],
            compiler_params=params(),
            cost_estimate=cost,
            name="item_terms",
        )(meta, tiles_in, words_in, fresh, turned, shards[key])

    if direct:
        arrived = [swap_row(item_terms(k, jnp.bfloat16), k) for k in range(n_row - 1, 0, -1)]
        item_grad = item_terms(0, jnp.float32)
        for part in arrived:
            item_grad = item_grad + part.astype(jnp.float32)
    else:
        item_grad = lax.psum_scatter(
            item_terms(0, jnp.float32), "row", scatter_dimension=0, tiled=True
        )
    values = items.astype(jnp.float32)
    items_new = (values - 0.005 * (item_grad + 0.05 * values)).astype(jnp.bfloat16)
    return (users_new, items_new)


def solution(mesh):
    return jax.shard_map(
        functools.partial(body, mesh.shape["row"], mesh.shape["col"]),
        mesh=mesh,
        in_specs=(
            P(("groups", "row", "col"), None),
            P(("groups", "row", "col"), None),
            P(("groups", "row"), "col", None, None, None),
            P(("groups", "row"), "col", None, None, None),
            P(("groups", "row"), "col", None),
            P(("groups", "row"), "col", None),
            P(("groups", "row"), "col"),
        ),
        out_specs=(P(("groups", "row", "col"), None), P(("groups", "row", "col"), None)),
        check_vma=False,
    )
```

```python
import functools

import jax
import jax.numpy as jnp
from jax import lax
from jax.experimental import pallas as pl
from jax.experimental.pallas import tpu as pltpu
from jax.sharding import PartitionSpec as P

BLOCK = 128
UNROLL = 16
FIELD = 10
VMEM_LIMIT = 16 * 1024 * 1024
PLAN_LIMIT = 50 * 1024 * 1024

NN = (((1,), (0,)), ((), ()))

vmem = functools.partial(pl.BlockSpec, memory_space=pltpu.VMEM)
smem = functools.partial(pl.BlockSpec, memory_space=pltpu.SMEM)
anywhere = functools.partial(pl.BlockSpec, memory_space=pl.ANY)


def params(limit=VMEM_LIMIT):
    return pltpu.CompilerParams(vmem_limit_bytes=limit)


def dot(a, b):
    return lax.dot_general(a, b, NN, preferred_element_type=jnp.float32)


def rows_of(index):
    return pl.ds(pl.multiple_of(index * BLOCK, BLOCK), BLOCK)


def tile(index):
    return slice(index * BLOCK, (index + 1) * BLOCK)


def plan_kernel(
    shard_tiles, group, stages, info, rows, cols, ratings, observed, meta, tiles, words, sems
):
    copy_tiles = pltpu.make_async_copy(ratings, tiles, sems.at[0])
    copy_words = pltpu.make_async_copy(observed, words, sems.at[1])
    copy_tiles.start()
    copy_words.start()
    count = info[0]
    me = info[1]
    ends = meta.shape[0] - 2

    def put(t, places):
        low, high = places
        v = cols[t]
        near = jnp.int32(1)
        if stages > 1:
            key = jnp.bitwise_xor(v // shard_tiles, me)
            near = jnp.where(key < group, 1, 0)
            v = (key % group) * shard_tiles + v % shard_tiles
        meta[jnp.where(near == 1, low, high)] = t + (rows[t] << FIELD) + (v << 2 * FIELD)
        return low + near, high - 1 + near

    low, _ = lax.fori_loop(0, count, put, (jnp.int32(0), count - 1))
    for at in range(UNROLL):
        meta[count + at] = 0
    meta[ends] = low
    meta[ends + 1] = count
    copy_tiles.wait()
    copy_words.wait()


def stage_loop(stage, meta, step_of):
    ends = meta.shape[0] - 2
    low = meta[ends] if stage else 0
    high = meta[ends + stage]
    mask = (1 << FIELD) - 1

    def step(i, _):
        entries = []
        for j in range(UNROLL):
            at = low + i * UNROLL + j
            word = meta[at]
            entries.append(
                (word & mask, (word >> FIELD) & mask, word >> 2 * FIELD, at < high)
            )
        step_of(entries)
        return _

    lax.fori_loop(0, (high - low + UNROLL - 1) // UNROLL, step, 0)


def masked_residual(predicted, tiles, words, slot, live):
    bit = jnp.left_shift(1, lax.broadcasted_iota(jnp.int32, (8, BLOCK), 0))
    bit = jnp.where(live, bit, 0)
    parts = []
    for w in range(BLOCK // 8):
        seen = jnp.broadcast_to(words[slot, pl.ds(w, 1), :], (8, BLOCK)) & bit
        gap = predicted[8 * w : 8 * w + 8] - tiles[slot, pl.ds(8 * w, 8), :].astype(jnp.float32)
        parts.append(jnp.where(seen != 0, gap, 0.0))
    return jnp.concatenate(parts, axis=0).astype(jnp.bfloat16)


def lay_items(shards, panel, flipped):
    per = shards[0].shape[0] // BLOCK
    for s, shard in enumerate(shards):
        for v in range(per):
            block = shard[tile(v)]
            panel[tile(s * per + v)] = block
            flipped[tile(s * per + v)] = block.T


def user_kernel(stage, group, last, *refs):
    if stage == 0:
        info, meta, tiles, words, mine, theirs = refs[:6]
        shards = refs[6 : 6 + group]
        users, flipped, total = refs[6 + group : 9 + group]
        count = mine.shape[0]
        lead = info[2] == 0
        users[:count] = jnp.where(lead, mine[...], theirs[...])
        users[count:] = jnp.where(lead, theirs[...], mine[...])
        total[...] = jnp.zeros_like(total)
    else:
        meta, tiles, words, users = refs[:4]
        shards = refs[4 : 4 + group]
        flipped, total = refs[5 + group : 7 + group]
    panel = refs[-1]
    lay_items(shards, panel, flipped)

    def step_of(entries):
        terms = []
        for slot, u, v, live in entries:
            predicted = dot(users[rows_of(u), :], flipped[rows_of(v), :])
            residual = masked_residual(predicted, tiles, words, slot, live)
            terms.append(dot(residual, panel[rows_of(v), :]))
        for (slot, u, v, live), term in zip(entries, terms):
            total[rows_of(u), :] += term

    stage_loop(stage, meta, step_of)
    if last:
        refs[-2][...] = total[...].astype(jnp.bfloat16)


def item_kernel(stage, group, first, *refs):
    if first:
        meta, tiles, words, mine, theirs, users, flipped = refs[:7]
        outs = refs[7 : 7 + group]
        fresh, turned = refs[7 + group : 9 + group]
        for u in range(users.shape[0] // BLOCK):
            values = users[tile(u)].astype(jnp.float32)
            gradient = mine[tile(u)].astype(jnp.float32) + theirs[tile(u)].astype(jnp.float32)
            new = (values - 0.02 * (gradient + 0.05 * values)).astype(jnp.bfloat16)
            fresh[tile(u)] = new
            turned[tile(u)] = new.T
    else:
        meta, tiles, words, fresh, turned, flipped = refs[:6]
        outs = refs[6 : 6 + group]
    total = refs[-1]
    total[...] = jnp.zeros_like(total)

    def step_of(entries):
        terms = []
        for slot, u, v, live in entries:
            predicted = dot(fresh[rows_of(u), :], flipped[rows_of(v), :])
            residual = masked_residual(predicted, tiles, words, slot, live)
            terms.append(dot(turned[rows_of(u), :], residual))
        for (slot, u, v, live), term in zip(entries, terms):
            total[rows_of(v), :] += term

    stage_loop(stage, meta, step_of)
    size = outs[0].shape[0]
    for s, out in enumerate(outs):
        out[...] = total[s * size : (s + 1) * size].astype(out.dtype)


def finish_kernel(items, *refs):
    out = refs[-1]
    for v in range(items.shape[0] // BLOCK):
        gradient = refs[0][tile(v)].astype(jnp.float32)
        for part in refs[1:-1]:
            gradient = gradient + part[tile(v)].astype(jnp.float32)
        values = items[tile(v)].astype(jnp.float32)
        out[tile(v)] = (values - 0.005 * (gradient.T + 0.05 * values)).astype(jnp.bfloat16)


def body(n_row, n_col, users, items, ratings, observed, tile_rows, tile_cols, tile_count):
    tiles = ratings[0, 0]
    words = observed[0, 0]
    slots = tiles.shape[0]
    rank = users.shape[-1]
    pad = slots + UNROLL
    direct = items.shape[0] % BLOCK == 0 and n_row & (n_row - 1) == 0 and n_row > 1
    stages = 2 if direct else 1
    group = n_row // 2 if direct else 1
    row_at = lax.axis_index("row")
    col_at = lax.axis_index("col")

    def swap_row(x, k):
        return lax.ppermute(x, "row", [(i, i ^ k) for i in range(n_row)])

    def swap_col(x):
        return lax.ppermute(x, "col", [(i, i ^ 1) for i in range(n_col)])

    peer_users = swap_col(users)
    if direct:
        crossed = swap_row(items, group)
        shards = [
            [items] + [swap_row(items, k) for k in range(1, group)],
            [crossed] + [swap_row(crossed, k) for k in range(1, group)],
        ]
    else:
        shards = [[lax.all_gather(items, "row", axis=0, tiled=True)]]
    wide = shards[0][0].shape[0]

    info = jnp.stack([tile_count[0, 0], row_at, col_at]).astype(jnp.int32)
    meta, tiles, words = pl.pallas_call(
        functools.partial(plan_kernel, wide // BLOCK, group, stages),
        out_shape=(
            jax.ShapeDtypeStruct((pad + 2,), jnp.int32),
            pltpu.VMEM(tiles.shape, tiles.dtype),
            pltpu.VMEM(words.shape, words.dtype),
        ),
        in_specs=[smem()] * 3 + [anywhere()] * 2,
        out_specs=(smem(), vmem(), vmem()),
        scratch_shapes=[pltpu.SemaphoreType.DMA((2,))],
        compiler_params=params(PLAN_LIMIT),
        name="plan",
    )(info, tile_rows[0, 0], tile_cols[0, 0], tiles, words)

    cost = pl.CostEstimate(
        flops=4 * slots * BLOCK * BLOCK * rank // stages,
        bytes_accessed=(slots // stages) * BLOCK * BLOCK * 4,
        transcendentals=0,
    )
    user_shape = (n_col * users.shape[0], rank)
    panel_shape = (group * wide, rank)
    flipped = []
    for stage in range(stages):
        last = stage == stages - 1
        shapes = [pltpu.VMEM(panel_shape, jnp.bfloat16), pltpu.VMEM(user_shape, jnp.float32)]
        if stage == 0:
            operands = [info, meta, tiles, words, users, peer_users] + shards[0]
            shapes = [pltpu.VMEM(user_shape, jnp.bfloat16)] + shapes
            aliases = {}
        else:
            operands = [meta, tiles, words, panel] + shards[stage] + [total]
            aliases = {len(operands) - 1: 1}
        if last:
            shapes.append(jax.ShapeDtypeStruct(user_shape, jnp.bfloat16))
        scalars = 2 if stage == 0 else 1
        outs = list(pl.pallas_call(
            functools.partial(user_kernel, stage, group, last),
            out_shape=tuple(shapes),
            in_specs=[smem()] * scalars + [vmem()] * (len(operands) - scalars),
            out_specs=tuple([vmem()] * len(shapes)),
            input_output_aliases=aliases,
            scratch_shapes=[pltpu.VMEM(panel_shape, jnp.bfloat16)],
            compiler_params=params(),
            cost_estimate=cost,
            name="user_terms",
        )(*operands))
        if stage == 0:
            panel = outs.pop(0)
        flipped.append(outs[0])
        total = outs[1]
    terms = outs[-1]
    peer_terms = swap_col(terms)

    fresh = turned = None
    sums = [None] * stages
    for stage in range(stages - 1, -1, -1):
        first = fresh is None
        shapes = [jax.ShapeDtypeStruct((wide, rank), jnp.float32)]
        shapes += [jax.ShapeDtypeStruct((wide, rank), jnp.bfloat16)] * (group - 1)
        if first:
            operands = [meta, tiles, words, terms, peer_terms, panel, flipped[stage]]
            shapes += [pltpu.VMEM(user_shape, jnp.bfloat16)] * 2
        else:
            operands = [meta, tiles, words, fresh, turned, flipped[stage]]
        outs = pl.pallas_call(
            functools.partial(item_kernel, stage, group, first),
            out_shape=tuple(shapes),
            in_specs=[smem()] + [vmem()] * (len(operands) - 1),
            out_specs=tuple([vmem()] * len(shapes)),
            scratch_shapes=[pltpu.VMEM(panel_shape, jnp.float32)],
            compiler_params=params(),
            cost_estimate=cost,
            name="item_terms",
        )(*operands)
        if first:
            fresh, turned = outs[group:]
        sums[stage] = [outs[0]] + [swap_row(outs[k], k) for k in range(1, group)]
    users_new = lax.dynamic_slice_in_dim(fresh, col_at * users.shape[0], users.shape[0], 0)

    if direct:
        relay = sums[1][0]
        for part in sums[1][1:]:
            relay = relay + part.astype(jnp.float32)
        parts = sums[0] + [swap_row(relay.astype(jnp.bfloat16), group)]
        items_new = pl.pallas_call(
            finish_kernel,
            out_shape=jax.ShapeDtypeStruct(items.shape, jnp.bfloat16),
            in_specs=[vmem()] * (1 + len(parts)),
            out_specs=vmem(),
            compiler_params=params(),
            name="finish",
        )(items, *parts)
    else:
        turned_terms = jnp.swapaxes(sums[0][0].reshape(-1, BLOCK, BLOCK), 1, 2)
        item_grad = lax.psum_scatter(
            turned_terms.reshape(wide, rank), "row", scatter_dimension=0, tiled=True
        )
        values = items.astype(jnp.float32)
        items_new = (values - 0.005 * (item_grad + 0.05 * values)).astype(jnp.bfloat16)
    return (users_new, items_new)


def solution(mesh):
    return jax.shard_map(
        functools.partial(body, mesh.shape["row"], mesh.shape["col"]),
        mesh=mesh,
        in_specs=(
            P(("groups", "row", "col"), None),
            P(("groups", "row", "col"), None),
            P(("groups", "row"), "col", None, None, None),
            P(("groups", "row"), "col", None, None, None),
            P(("groups", "row"), "col", None),
            P(("groups", "row"), "col", None),
            P(("groups", "row"), "col"),
        ),
        out_specs=(P(("groups", "row", "col"), None), P(("groups", "row", "col"), None)),
        check_vma=False,
    )
```

```python
import functools

import jax
import jax.numpy as jnp
from jax import lax
from jax.experimental import pallas as pl
from jax.experimental.pallas import tpu as pltpu
from jax.sharding import PartitionSpec as P

BLOCK = 128
UNROLL = 16
FIELD = 10
PLAN_UNROLL = 8
VMEM_LIMIT = 16 * 1024 * 1024
PLAN_LIMIT = 50 * 1024 * 1024

NN = (((1,), (0,)), ((), ()))

vmem = functools.partial(pl.BlockSpec, memory_space=pltpu.VMEM)
smem = functools.partial(pl.BlockSpec, memory_space=pltpu.SMEM)
anywhere = functools.partial(pl.BlockSpec, memory_space=pl.ANY)


def params(limit=VMEM_LIMIT):
    return pltpu.CompilerParams(vmem_limit_bytes=limit)


def dot(a, b):
    return lax.dot_general(a, b, NN, preferred_element_type=jnp.float32)


def rows_of(index):
    return pl.ds(pl.multiple_of(index * BLOCK, BLOCK), BLOCK)


def tile(index):
    return slice(index * BLOCK, (index + 1) * BLOCK)


def plan_kernel(shard_tiles, group, stages, live, rows, cols, meta):
    count = live[0, 0]
    me = lax.axis_index("row")
    ends = meta.shape[0] - 2
    spare = meta.shape[0] - 3

    def put(i, places):
        low, high = places
        packed = []
        for j in range(PLAN_UNROLL):
            t = i * PLAN_UNROLL + j
            at = jnp.minimum(t, rows.shape[0] - 1)
            v = cols[at]
            near = jnp.int32(1)
            if stages > 1:
                key = (v ^ (me * shard_tiles)) & (2 * group * shard_tiles - 1)
                near = jnp.where(key < (group + 1) * shard_tiles, 1, 0)
                v = jnp.where(near == 1, key, key - (group + 1) * shard_tiles)
            packed.append((t, near, at + (rows[at] << FIELD) + (v << 2 * FIELD)))
        for t, near, word in packed:
            live = jnp.where(t < count, 1, 0)
            meta[jnp.where(live == 0, spare, jnp.where(near == 1, low, high))] = word
            low = low + near * live
            high = high - (1 - near) * live
        return low, high

    trips = (count + PLAN_UNROLL - 1) // PLAN_UNROLL
    low, _ = lax.fori_loop(0, trips, put, (jnp.int32(0), count - 1))
    for at in range(UNROLL):
        meta[count + at] = 0
    meta[ends] = low
    meta[ends + 1] = count


def stage_loop(stage, meta, step_of):
    ends = meta.shape[0] - 2
    low = meta[ends] if stage else 0
    high = meta[ends + stage]
    mask = (1 << FIELD) - 1

    def step(i, _):
        entries = []
        for j in range(UNROLL):
            at = low + i * UNROLL + j
            word = meta[at]
            entries.append(
                (word & mask, (word >> FIELD) & mask, word >> 2 * FIELD, at < high)
            )
        step_of(entries)
        return _

    lax.fori_loop(0, (high - low + UNROLL - 1) // UNROLL, step, 0)


def masked_residual(predicted, tiles, words, slot, live):
    bit = jnp.left_shift(1, lax.broadcasted_iota(jnp.int32, (8, BLOCK), 0))
    bit = jnp.where(live, bit, 0)
    parts = []
    for w in range(BLOCK // 8):
        seen = jnp.broadcast_to(words[slot, pl.ds(w, 1), :], (8, BLOCK)) & bit
        gap = predicted[8 * w : 8 * w + 8] - tiles[slot, pl.ds(8 * w, 8), :].astype(jnp.float32)
        parts.append(jnp.where(seen != 0, gap, 0.0))
    return jnp.concatenate(parts, axis=0).astype(jnp.bfloat16)


def lay_items(shards, panel, flipped):
    per = shards[0].shape[0] // BLOCK
    for s, shard in enumerate(shards):
        for v in range(per):
            block = shard[tile(v)]
            panel[tile(s * per + v)] = block
            flipped[tile(s * per + v)] = block.T


def user_kernel(stage, group, last, *refs):
    if stage == 0:
        meta, tiles, words, mine, theirs = refs[:5]
        shards = refs[5 : 5 + group]
        users, flipped, total = refs[5 + group : 8 + group]
        count = mine.shape[0]
        lead = lax.axis_index("col") == 0
        users[:count] = jnp.where(lead, mine[...], theirs[...])
        users[count:] = jnp.where(lead, theirs[...], mine[...])
        total[...] = jnp.zeros_like(total)
    else:
        meta, tiles, words, users = refs[:4]
        shards = refs[4 : 4 + group]
        flipped, total = refs[5 + group : 7 + group]
    panel = refs[-1]
    lay_items(shards, panel, flipped)

    def step_of(entries):
        terms = []
        for slot, u, v, live in entries:
            predicted = dot(users[rows_of(u), :], flipped[rows_of(v), :])
            residual = masked_residual(predicted, tiles, words, slot, live)
            terms.append(dot(residual, panel[rows_of(v), :]))
        for (slot, u, v, live), term in zip(entries, terms):
            total[rows_of(u), :] += term

    stage_loop(stage, meta, step_of)
    if last:
        refs[-2][...] = total[...].astype(jnp.bfloat16)


def item_kernel(stage, group, first, *refs):
    if first:
        meta, tiles, words, mine, theirs, users, flipped = refs[:7]
        outs = refs[7 : 7 + group]
        fresh, turned = refs[7 + group : 9 + group]
        for u in range(users.shape[0] // BLOCK):
            values = users[tile(u)].astype(jnp.float32)
            gradient = mine[tile(u)].astype(jnp.float32) + theirs[tile(u)].astype(jnp.float32)
            new = (values - 0.02 * (gradient + 0.05 * values)).astype(jnp.bfloat16)
            fresh[tile(u)] = new
            turned[tile(u)] = new.T
    else:
        meta, tiles, words, fresh, turned, flipped = refs[:6]
        outs = refs[6 : 6 + group]
    total = refs[-1]
    total[...] = jnp.zeros_like(total)

    def step_of(entries):
        terms = []
        for slot, u, v, live in entries:
            predicted = dot(fresh[rows_of(u), :], flipped[rows_of(v), :])
            residual = masked_residual(predicted, tiles, words, slot, live)
            terms.append(dot(turned[rows_of(u), :], residual))
        for (slot, u, v, live), term in zip(entries, terms):
            total[rows_of(v), :] += term

    stage_loop(stage, meta, step_of)
    size = outs[0].shape[0]
    for s, out in enumerate(outs):
        out[...] = total[s * size : (s + 1) * size].astype(out.dtype)


def finish_kernel(items, *refs):
    out = refs[-1]
    for v in range(items.shape[0] // BLOCK):
        gradient = refs[0][tile(v)].astype(jnp.float32)
        for part in refs[1:-1]:
            gradient = gradient + part[tile(v)].astype(jnp.float32)
        values = items[tile(v)].astype(jnp.float32)
        out[tile(v)] = (values - 0.005 * (gradient.T + 0.05 * values)).astype(jnp.bfloat16)


def body(n_row, n_col, users, items, ratings, observed, tile_rows, tile_cols, tile_count):
    tiles = ratings[0, 0]
    words = observed[0, 0]
    slots = tiles.shape[0]
    rank = users.shape[-1]
    pad = slots + UNROLL
    per = items.shape[0] // BLOCK
    direct = items.shape[0] == per * BLOCK and n_row > 2
    direct = direct and (n_row & (n_row - 1)) == 0 and (per & (per - 1)) == 0
    stages = 2 if direct else 1
    group = n_row // 2 if direct else 1
    col_at = lax.axis_index("col")

    def swap_row(x, k):
        return lax.ppermute(x, "row", [(i, i ^ k) for i in range(n_row)])

    def swap_col(x):
        return lax.ppermute(x, "col", [(i, i ^ 1) for i in range(n_col)])

    peer_users = swap_col(users)
    if direct:
        crossed = swap_row(items, group)
        shards = [[items] + [swap_row(items, k) for k in range(1, group)]]
    else:
        shards = [[lax.all_gather(items, "row", axis=0, tiled=True)]]
    wide = shards[0][0].shape[0]

    meta = pl.pallas_call(
        functools.partial(plan_kernel, wide // BLOCK, group, stages),
        out_shape=pltpu.SMEM((pad + 3,), jnp.int32),
        in_specs=[smem()] * 3,
        out_specs=smem(),
        compiler_params=params(),
        cost_estimate=pl.CostEstimate(flops=10**10, bytes_accessed=0, transcendentals=0),
        name="plan",
    )(tile_count, tile_rows[0, 0], tile_cols[0, 0])

    if direct:
        crossed, meta = lax.optimization_barrier((crossed, meta))
        shards[0].append(crossed)
        shards.append([swap_row(crossed, k) for k in range(1, group)])

    cost = pl.CostEstimate(
        flops=20 * slots * BLOCK * BLOCK * rank // stages,
        bytes_accessed=(slots // stages) * BLOCK * BLOCK * 4,
        transcendentals=0,
    )
    user_shape = (n_col * users.shape[0], rank)
    flipped = []
    for stage in range(stages):
        size = len(shards[stage])
        panel_shape = (size * wide, rank)
        last = stage == stages - 1
        shapes = [pltpu.VMEM(panel_shape, jnp.bfloat16), pltpu.VMEM(user_shape, jnp.float32)]
        if stage == 0:
            operands = [meta, tiles, words, users, peer_users] + shards[0]
            shapes = [pltpu.VMEM(user_shape, jnp.bfloat16)] + shapes
            aliases = {}
        else:
            operands = [meta, tiles, words, panel] + shards[stage] + [total]
            aliases = {len(operands) - 1: 1}
        if last:
            shapes.append(jax.ShapeDtypeStruct(user_shape, jnp.bfloat16))
        outs = list(pl.pallas_call(
            functools.partial(user_kernel, stage, size, last),
            out_shape=tuple(shapes),
            in_specs=[smem()] + [vmem()] * (len(operands) - 1),
            out_specs=tuple([vmem()] * len(shapes)),
            input_output_aliases=aliases,
            scratch_shapes=[pltpu.VMEM(panel_shape, jnp.bfloat16)],
            compiler_params=params(),
            cost_estimate=cost,
            name="user_terms",
        )(*operands))
        if stage == 0:
            panel = outs.pop(0)
        flipped.append(outs[0])
        total = outs[1]
    terms = outs[-1]
    peer_terms = swap_col(terms)

    fresh = turned = None
    for stage in range(stages - 1, -1, -1):
        first = fresh is None
        size = len(shards[stage])
        kinds = [jnp.bfloat16] * size
        if stage == 0:
            kinds[0] = kinds[-1] = jnp.float32
        shapes = [jax.ShapeDtypeStruct((wide, rank), kind) for kind in kinds]
        if first:
            operands = [meta, tiles, words, terms, peer_terms, panel, flipped[stage]]
            shapes += [pltpu.VMEM(user_shape, jnp.bfloat16)] * 2
        else:
            operands = [meta, tiles, words, fresh, turned, flipped[stage]]
        outs = pl.pallas_call(
            functools.partial(item_kernel, stage, size, first),
            out_shape=tuple(shapes),
            in_specs=[smem()] + [vmem()] * (len(operands) - 1),
            out_specs=tuple([vmem()] * len(shapes)),
            scratch_shapes=[pltpu.VMEM((size * wide, rank), jnp.float32)],
            compiler_params=params(),
            cost_estimate=cost,
            name="item_terms",
        )(*operands)
        if first:
            fresh, turned = outs[size:]
        if stage:
            far = [swap_row(out, k + 1) for k, out in enumerate(outs[:size])]
        else:
            near = [outs[0]] + [swap_row(outs[k], k) for k in range(1, group)]
            relay = outs[size - 1]
    users_new = lax.dynamic_slice_in_dim(fresh, col_at * users.shape[0], users.shape[0], 0)

    if direct:
        for part in far:
            relay = relay + part.astype(jnp.float32)
        parts = near + [swap_row(relay.astype(jnp.bfloat16), group)]
        items_new = pl.pallas_call(
            finish_kernel,
            out_shape=jax.ShapeDtypeStruct(items.shape, jnp.bfloat16),
            in_specs=[vmem()] * (1 + len(parts)),
            out_specs=vmem(),
            compiler_params=params(),
            name="finish",
        )(items, *parts)
    else:
        turned_terms = jnp.swapaxes(near[0].reshape(-1, BLOCK, BLOCK), 1, 2)
        item_grad = lax.psum_scatter(
            turned_terms.reshape(wide, rank), "row", scatter_dimension=0, tiled=True
        )
        values = items.astype(jnp.float32)
        items_new = (values - 0.005 * (item_grad + 0.05 * values)).astype(jnp.bfloat16)
    return (users_new, items_new)


def solution(mesh):
    return jax.shard_map(
        functools.partial(body, mesh.shape["row"], mesh.shape["col"]),
        mesh=mesh,
        in_specs=(
            P(("groups", "row", "col"), None),
            P(("groups", "row", "col"), None),
            P(("groups", "row"), "col", None, None, None),
            P(("groups", "row"), "col", None, None, None),
            P(("groups", "row"), "col", None),
            P(("groups", "row"), "col", None),
            P(("groups", "row"), "col"),
        ),
        out_specs=(P(("groups", "row", "col"), None), P(("groups", "row", "col"), None)),
        check_vma=False,
    )
```

```python
import functools

import jax
import jax.numpy as jnp
from jax import lax
from jax.experimental import pallas as pl
from jax.experimental.pallas import tpu as pltpu
from jax.sharding import PartitionSpec as P

BLOCK = 128
UNROLL = 24
TAIL = 8
FIELD = 10
PLAN_UNROLL = 8
VMEM_LIMIT = 16 * 1024 * 1024

NN = (((1,), (0,)), ((), ()))

vmem = functools.partial(pl.BlockSpec, memory_space=pltpu.VMEM)
smem = functools.partial(pl.BlockSpec, memory_space=pltpu.SMEM)
anywhere = functools.partial(pl.BlockSpec, memory_space=pl.ANY)


def params(limit=VMEM_LIMIT):
    return pltpu.CompilerParams(vmem_limit_bytes=limit)


def dot(a, b):
    return lax.dot_general(a, b, NN, preferred_element_type=jnp.float32)


def rows_of(index):
    return pl.ds(pl.multiple_of(index * BLOCK, BLOCK), BLOCK)


def tile(index):
    return slice(index * BLOCK, (index + 1) * BLOCK)


def plan_kernel(shard_tiles, keys, edges, live, rows, cols, total, meta):
    count = live[0, 0]
    me = lax.axis_index("row")
    stages = len(edges)
    region = (meta.shape[0] - stages) // stages

    def put(i, places):
        places = list(places)
        packed = []
        for j in range(PLAN_UNROLL):
            t = i * PLAN_UNROLL + j
            at = jnp.minimum(t, rows.shape[0] - 1)
            v = cols[at]
            if stages > 1:
                v = (v ^ (me * shard_tiles)) & (keys * shard_tiles - 1)
            packed.append((t, v, at + (rows[at] << FIELD)))
        for t, v, word in packed:
            spot, base = places[0], jnp.int32(0)
            inside = [v < edges[0]]
            for stage in range(1, stages):
                past = v >= edges[stage - 1]
                spot = jnp.where(past, stage * region + places[stage], spot)
                base = jnp.where(past, edges[stage - 1], base)
                inside.append(past & (v < edges[stage]))
            meta[spot] = word + ((v - base) << 2 * FIELD)
            for stage in range(stages):
                places[stage] += jnp.where(inside[stage] & (t < count), 1, 0)
        return tuple(places)

    trips = (count + PLAN_UNROLL - 1) // PLAN_UNROLL
    places = lax.fori_loop(0, trips, put, (jnp.int32(0),) * stages)
    for stage in range(stages):
        for at in range(UNROLL):
            meta[stage * region + places[stage] + at] = 0
        meta[stages * region + stage] = places[stage]


def stage_loop(stage, stages, meta, step_of):
    region = (meta.shape[0] - stages) // stages
    live = meta[stages * region + stage]
    mask = (1 << FIELD) - 1

    def group(start, size):
        entries = []
        for j in range(size):
            at = start + j
            word = meta[stage * region + at]
            entries.append(
                (word & mask, (word >> FIELD) & mask, word >> 2 * FIELD, at < live)
            )
        step_of(entries)

    def step(i, _):
        group(i * UNROLL, UNROLL)
        return _

    whole = (live + UNROLL - TAIL - 1) // UNROLL
    lax.fori_loop(0, whole, step, 0)

    @pl.when(whole * UNROLL < live)
    def _():
        group(whole * UNROLL, TAIL)


def masked_residual(predicted, tiles, words, slot, live):
    bit = jnp.left_shift(1, lax.broadcasted_iota(jnp.int32, (8, BLOCK), 0))
    bit = jnp.where(live, bit, 0)
    parts = []
    for w in range(BLOCK // 8):
        seen = jnp.broadcast_to(words[slot, pl.ds(w, 1), :], (8, BLOCK)) & bit
        gap = predicted[8 * w : 8 * w + 8] - tiles[slot, pl.ds(8 * w, 8), :].astype(jnp.float32)
        parts.append(jnp.where(seen != 0, gap, 0.0))
    return jnp.concatenate(parts, axis=0).astype(jnp.bfloat16)


def lay_items(shards, panel, flipped):
    per = shards[0].shape[0] // BLOCK
    for s, shard in enumerate(shards):
        for v in range(per):
            block = shard[tile(v)]
            panel[tile(s * per + v)] = block
            flipped[tile(s * per + v)] = block.T


def clear_kernel(total):
    total[...] = jnp.zeros_like(total)


def user_kernel(stage, stages, group, last, *refs):
    meta, tiles, words = refs[:3]
    shards = refs[3 : 3 + group]
    if stage == 0:
        mine, theirs = refs[3 + group : 5 + group]
        flipped, total, users = refs[6 + group : 9 + group]
        count = mine.shape[0]
        lead = lax.axis_index("col") == 0
        users[:count] = jnp.where(lead, mine[...], theirs[...])
        users[count:] = jnp.where(lead, theirs[...], mine[...])
    else:
        users = refs[3 + group]
        flipped, total = refs[5 + group : 7 + group]
    panel = refs[-1]
    lay_items(shards, panel, flipped)

    def step_of(entries):
        terms = []
        for slot, u, v, live in entries:
            predicted = dot(users[rows_of(u), :], flipped[rows_of(v), :])
            residual = masked_residual(predicted, tiles, words, slot, live)
            terms.append(dot(residual, panel[rows_of(v), :]))
        for (slot, u, v, live), term in zip(entries, terms):
            total[rows_of(u), :] += term

    stage_loop(stage, stages, meta, step_of)
    if last:
        refs[-2][...] = total[...].astype(jnp.bfloat16)


def item_kernel(parts, stages, first, *refs):
    meta, tiles, words = refs[:3]
    flips = refs[3 : 3 + len(parts)]
    refs = refs[3 + len(parts) :]
    total = refs[-1]
    if first:
        mine, theirs, users = refs[:3]
        outs = refs[3:-3]
        fresh, turned = refs[-3:-1]
        for u in range(users.shape[0] // BLOCK):
            values = users[tile(u)].astype(jnp.float32)
            gradient = mine[tile(u)].astype(jnp.float32) + theirs[tile(u)].astype(jnp.float32)
            new = (values - 0.02 * (gradient + 0.05 * values)).astype(jnp.bfloat16)
            fresh[tile(u)] = new
            turned[tile(u)] = new.T
    else:
        fresh, turned = refs[:2]
        outs = refs[2:-1]
    total[...] = jnp.zeros_like(total)
    base = 0
    for stage, flipped in zip(parts, flips):

        def step_of(entries, base=base, flipped=flipped):
            terms = []
            for slot, u, v, live in entries:
                predicted = dot(fresh[rows_of(u), :], flipped[rows_of(v), :])
                residual = masked_residual(predicted, tiles, words, slot, live)
                terms.append(dot(turned[rows_of(u), :], residual))
            for (slot, u, v, live), term in zip(entries, terms):
                total[rows_of(v + base), :] += term

        stage_loop(stage, stages, meta, step_of)
        base += flipped.shape[0] // BLOCK
    size = outs[0].shape[0]
    for s, out in enumerate(outs):
        out[...] = total[s * size : (s + 1) * size].astype(out.dtype)


def finish_kernel(items, *refs):
    out = refs[-1]
    for v in range(items.shape[0] // BLOCK):
        gradient = refs[0][tile(v)].astype(jnp.float32)
        for part in refs[1:-1]:
            gradient = gradient + part[tile(v)].astype(jnp.float32)
        values = items[tile(v)].astype(jnp.float32)
        out[tile(v)] = (values - 0.005 * (gradient.T + 0.05 * values)).astype(jnp.bfloat16)


def body(n_row, n_col, users, items, ratings, observed, tile_rows, tile_cols, tile_count):
    tiles = ratings[0, 0]
    words = observed[0, 0]
    slots = tiles.shape[0]
    rank = users.shape[-1]
    pad = slots + UNROLL
    per = items.shape[0] // BLOCK
    direct = items.shape[0] == per * BLOCK and n_row > 2
    direct = direct and (n_row & (n_row - 1)) == 0 and (per & (per - 1)) == 0
    keys = n_row if direct else 1
    half = n_row // 2
    groups = [[0]]
    if direct:
        groups = [list(range(half + 1)), list(range(half + 1, n_row))]
    stages = len(groups)
    col_at = lax.axis_index("col")

    def swap_row(x, k):
        return lax.ppermute(x, "row", [(i, i ^ k) for i in range(n_row)])

    def swap_col(x):
        return lax.ppermute(x, "col", [(i, i ^ 1) for i in range(n_col)])

    peer_users = swap_col(users)
    user_shape = (n_col * users.shape[0], rank)
    total = pl.pallas_call(
        clear_kernel,
        out_shape=pltpu.VMEM(user_shape, jnp.float32),
        out_specs=vmem(),
        compiler_params=params(),
        cost_estimate=pl.CostEstimate(flops=10**10, bytes_accessed=0, transcendentals=0),
        name="clear",
    )()
    shards = [items]
    if direct:
        shards += [swap_row(items, k) for k in range(1, half)]
        crossed = swap_row(items, half)
        shards += [crossed] + [swap_row(crossed, k) for k in range(1, half)]
    else:
        shards = [lax.all_gather(items, "row", axis=0, tiled=True)]
    wide = shards[0].shape[0]
    shard_tiles = wide // BLOCK
    edges = [(group[-1] + 1) * shard_tiles for group in groups]

    meta = pl.pallas_call(
        functools.partial(plan_kernel, shard_tiles, keys, edges),
        out_shape=pltpu.SMEM((stages * pad + stages,), jnp.int32),
        in_specs=[smem()] * 3 + [anywhere()],
        out_specs=smem(),
        compiler_params=params(),
        name="plan",
    )(tile_count, tile_rows[0, 0], tile_cols[0, 0], total)

    cost = pl.CostEstimate(
        flops=20 * slots * BLOCK * BLOCK * rank // stages,
        bytes_accessed=(slots // stages) * BLOCK * BLOCK * 4,
        transcendentals=0,
    )
    flipped = []
    for stage, group in enumerate(groups):
        last = stage == stages - 1
        size = len(group)
        panel_shape = (size * wide, rank)
        shapes = [pltpu.VMEM(panel_shape, jnp.bfloat16), pltpu.VMEM(user_shape, jnp.float32)]
        operands = [meta, tiles, words] + [shards[key] for key in group]
        operands += [users, peer_users, total] if stage == 0 else [panel, total]
        if stage == 0:
            shapes.append(pltpu.VMEM(user_shape, jnp.bfloat16))
        if last:
            shapes.append(jax.ShapeDtypeStruct(user_shape, jnp.bfloat16))
        outs = pl.pallas_call(
            functools.partial(user_kernel, stage, stages, size, last),
            out_shape=tuple(shapes),
            in_specs=[smem()] + [vmem()] * (len(operands) - 1),
            out_specs=tuple([vmem()] * len(shapes)),
            input_output_aliases={len(operands) - 1: 1},
            scratch_shapes=[pltpu.VMEM(panel_shape, jnp.bfloat16)],
            compiler_params=params(),
            cost_estimate=cost,
            name="user_terms",
        )(*operands)
        flipped.append(outs[0])
        total = outs[1]
        if stage == 0:
            panel = outs[2]
    terms = outs[-1]
    peer_terms = swap_col(terms)

    sums = [None] * keys
    for parts in ([range(1, stages)] if direct else []) + [range(1)]:
        first = 0 not in parts or not direct
        named = [key for stage in parts for key in groups[stage]]
        shapes = [
            jax.ShapeDtypeStruct(
                (wide, rank), jnp.float32 if key in (0, half) else jnp.bfloat16
            )
            for key in named
        ]
        operands = [meta, tiles, words] + [flipped[stage] for stage in parts]
        if first:
            operands += [terms, peer_terms, panel]
            shapes += [pltpu.VMEM(user_shape, jnp.bfloat16)] * 2
        else:
            operands += [fresh, turned]
        outs = pl.pallas_call(
            functools.partial(item_kernel, tuple(parts), stages, first),
            out_shape=tuple(shapes),
            in_specs=[smem()] + [vmem()] * (len(operands) - 1),
            out_specs=tuple([vmem()] * len(shapes)),
            scratch_shapes=[pltpu.VMEM((len(named) * wide, rank), jnp.float32)],
            compiler_params=params(),
            cost_estimate=cost,
            name="item_terms",
        )(*operands)
        if first:
            fresh, turned = outs[-2:]
        for key, out in zip(named, outs):
            sums[key] = out if key in (0, half) else swap_row(out, key % half)
    users_new = lax.dynamic_slice_in_dim(fresh, col_at * users.shape[0], users.shape[0], 0)

    if direct:
        relay = sums[half]
        for part in sums[half + 1 :]:
            relay = relay + part.astype(jnp.float32)
        parts = sums[:half] + [swap_row(relay.astype(jnp.bfloat16), half)]
        items_new = pl.pallas_call(
            finish_kernel,
            out_shape=jax.ShapeDtypeStruct(items.shape, jnp.bfloat16),
            in_specs=[vmem()] * (1 + len(parts)),
            out_specs=vmem(),
            compiler_params=params(),
            name="finish",
        )(items, *parts)
    else:
        turned_terms = jnp.swapaxes(sums[0].reshape(-1, BLOCK, BLOCK), 1, 2)
        item_grad = lax.psum_scatter(
            turned_terms.reshape(wide, rank), "row", scatter_dimension=0, tiled=True
        )
        values = items.astype(jnp.float32)
        items_new = (values - 0.005 * (item_grad + 0.05 * values)).astype(jnp.bfloat16)
    return (users_new, items_new)


def solution(mesh):
    return jax.shard_map(
        functools.partial(body, mesh.shape["row"], mesh.shape["col"]),
        mesh=mesh,
        in_specs=(
            P(("groups", "row", "col"), None),
            P(("groups", "row", "col"), None),
            P(("groups", "row"), "col", None, None, None),
            P(("groups", "row"), "col", None, None, None),
            P(("groups", "row"), "col", None),
            P(("groups", "row"), "col", None),
            P(("groups", "row"), "col"),
        ),
        out_specs=(P(("groups", "row", "col"), None), P(("groups", "row", "col"), None)),
        check_vma=False,
    )
```

```python
import functools

import jax
import jax.numpy as jnp
from jax import lax
from jax.experimental import pallas as pl
from jax.experimental.pallas import tpu as pltpu
from jax.sharding import PartitionSpec as P

BLOCK = 128
UNROLL = 24
TAIL = 8
FIELD = 10
PLAN_UNROLL = 8
VMEM_LIMIT = 16 * 1024 * 1024

NN = (((1,), (0,)), ((), ()))

vmem = functools.partial(pl.BlockSpec, memory_space=pltpu.VMEM)
smem = functools.partial(pl.BlockSpec, memory_space=pltpu.SMEM)
anywhere = functools.partial(pl.BlockSpec, memory_space=pl.ANY)


def params(limit=VMEM_LIMIT):
    return pltpu.CompilerParams(vmem_limit_bytes=limit)


def dot(a, b):
    return lax.dot_general(a, b, NN, preferred_element_type=jnp.float32)


def rows_of(index):
    return pl.ds(pl.multiple_of(index * BLOCK, BLOCK), BLOCK)


def tile(index):
    return slice(index * BLOCK, (index + 1) * BLOCK)


def plan_kernel(shard_tiles, keys, edges, live, rows, cols, total, meta):
    count = live[0, 0]
    me = lax.axis_index("row")
    stages = len(edges)
    region = (meta.shape[0] - stages) // stages

    def put(i, places):
        places = list(places)
        packed = []
        for j in range(PLAN_UNROLL):
            t = i * PLAN_UNROLL + j
            at = jnp.minimum(t, rows.shape[0] - 1)
            v = cols[at]
            if stages > 1:
                v = (v ^ (me * shard_tiles)) & (keys * shard_tiles - 1)
            packed.append((t, v, at + (rows[at] << FIELD)))
        for t, v, word in packed:
            spot, base = places[0], jnp.int32(0)
            inside = [v < edges[0]]
            for stage in range(1, stages):
                past = v >= edges[stage - 1]
                spot = jnp.where(past, stage * region + places[stage], spot)
                base = jnp.where(past, edges[stage - 1], base)
                inside.append(past & (v < edges[stage]))
            meta[spot] = word + ((v - base) << 2 * FIELD)
            for stage in range(stages):
                places[stage] += jnp.where(inside[stage] & (t < count), 1, 0)
        return tuple(places)

    trips = (count + PLAN_UNROLL - 1) // PLAN_UNROLL
    places = lax.fori_loop(0, trips, put, (jnp.int32(0),) * stages)
    for stage in range(stages):
        for at in range(UNROLL):
            meta[stage * region + places[stage] + at] = 0
        meta[stages * region + stage] = places[stage]


def stage_loop(stage, stages, meta, step_of):
    region = (meta.shape[0] - stages) // stages
    live = meta[stages * region + stage]
    mask = (1 << FIELD) - 1

    def group(start, size):
        entries = []
        for j in range(size):
            at = start + j
            word = meta[stage * region + at]
            entries.append(
                (word & mask, (word >> FIELD) & mask, word >> 2 * FIELD, at < live)
            )
        step_of(entries)

    def step(i, _):
        group(i * UNROLL, UNROLL)
        return _

    whole = (live + UNROLL - TAIL - 1) // UNROLL
    lax.fori_loop(0, whole, step, 0)

    @pl.when(whole * UNROLL < live)
    def _():
        group(whole * UNROLL, TAIL)


def masked_residual(predicted, tiles, words, slot, live):
    bit = jnp.left_shift(1, lax.broadcasted_iota(jnp.int32, (8, BLOCK), 0))
    bit = jnp.where(live, bit, 0)
    parts = []
    for w in range(BLOCK // 8):
        seen = jnp.broadcast_to(words[slot, pl.ds(w, 1), :], (8, BLOCK)) & bit
        gap = predicted[8 * w : 8 * w + 8] - tiles[slot, pl.ds(8 * w, 8), :].astype(jnp.float32)
        parts.append(jnp.where(seen != 0, gap, 0.0))
    return jnp.concatenate(parts, axis=0).astype(jnp.bfloat16)


def lay_items(shards, panel, flipped):
    per = shards[0].shape[0] // BLOCK
    for s, shard in enumerate(shards):
        for v in range(per):
            block = shard[tile(v)]
            panel[tile(s * per + v)] = block
            flipped[tile(s * per + v)] = block.T


def clear_kernel(total):
    total[...] = jnp.zeros_like(total)


def user_kernel(stage, stages, group, last, *refs):
    meta, tiles, words = refs[:3]
    shards = refs[3 : 3 + group]
    if stage == 0:
        mine, theirs = refs[3 + group : 5 + group]
        flipped, total, users = refs[6 + group : 9 + group]
        count = mine.shape[0]
        lead = lax.axis_index("col") == 0
        users[:count] = jnp.where(lead, mine[...], theirs[...])
        users[count:] = jnp.where(lead, theirs[...], mine[...])
    else:
        users = refs[3 + group]
        flipped, total = refs[5 + group : 7 + group]
    panel = refs[-1]
    lay_items(shards, panel, flipped)

    def step_of(entries):
        terms = []
        for slot, u, v, live in entries:
            predicted = dot(users[rows_of(u), :], flipped[rows_of(v), :])
            residual = masked_residual(predicted, tiles, words, slot, live)
            terms.append(dot(residual, panel[rows_of(v), :]))
        for (slot, u, v, live), term in zip(entries, terms):
            total[rows_of(u), :] += term

    stage_loop(stage, stages, meta, step_of)
    if last:
        refs[-2][...] = total[...].astype(jnp.bfloat16)


def item_kernel(parts, stages, first, *refs):
    meta, tiles, words = refs[:3]
    flips = refs[3 : 3 + len(parts)]
    refs = refs[3 + len(parts) :]
    total = refs[-1]
    if first:
        mine, theirs, users = refs[:3]
        outs = refs[3:-3]
        fresh, turned = refs[-3:-1]
        for u in range(users.shape[0] // BLOCK):
            values = users[tile(u)].astype(jnp.float32)
            gradient = mine[tile(u)].astype(jnp.float32) + theirs[tile(u)].astype(jnp.float32)
            new = (values - 0.02 * (gradient + 0.05 * values)).astype(jnp.bfloat16)
            fresh[tile(u)] = new
            turned[tile(u)] = new.T
    else:
        fresh, turned = refs[:2]
        outs = refs[2:-1]
    total[...] = jnp.zeros_like(total)
    base = 0
    for stage, flipped in zip(parts, flips):

        def step_of(entries, base=base, flipped=flipped):
            terms = []
            for slot, u, v, live in entries:
                predicted = dot(fresh[rows_of(u), :], flipped[rows_of(v), :])
                residual = masked_residual(predicted, tiles, words, slot, live)
                terms.append(dot(turned[rows_of(u), :], residual))
            for (slot, u, v, live), term in zip(entries, terms):
                total[rows_of(v + base), :] += term

        stage_loop(stage, stages, meta, step_of)
        base += flipped.shape[0] // BLOCK
    size = outs[0].shape[0]
    for s, out in enumerate(outs):
        out[...] = total[s * size : (s + 1) * size].astype(out.dtype)


def finish_kernel(items, *refs):
    out = refs[-1]
    for v in range(items.shape[0] // BLOCK):
        gradient = refs[0][tile(v)].astype(jnp.float32)
        for part in refs[1:-1]:
            gradient = gradient + part[tile(v)].astype(jnp.float32)
        values = items[tile(v)].astype(jnp.float32)
        out[tile(v)] = (values - 0.005 * (gradient.T + 0.05 * values)).astype(jnp.bfloat16)


def body(n_row, n_col, users, items, ratings, observed, tile_rows, tile_cols, tile_count):
    tiles = ratings[0, 0]
    words = observed[0, 0]
    slots = tiles.shape[0]
    rank = users.shape[-1]
    pad = slots + UNROLL
    per = items.shape[0] // BLOCK
    direct = items.shape[0] == per * BLOCK and n_row > 2
    direct = direct and (n_row & (n_row - 1)) == 0 and (per & (per - 1)) == 0
    keys = n_row if direct else 1
    half = n_row // 2
    groups = [[0]]
    if direct:
        groups = [range(half + 1), range(half + 1, n_row - 1), range(n_row - 1, n_row)]
        groups = [list(group) for group in groups if len(group)]
    stages = len(groups)
    col_at = lax.axis_index("col")

    def swap_row(x, k):
        return lax.ppermute(x, "row", [(i, i ^ k) for i in range(n_row)])

    def swap_col(x):
        return lax.ppermute(x, "col", [(i, i ^ 1) for i in range(n_col)])

    peer_users = swap_col(users)
    user_shape = (n_col * users.shape[0], rank)
    total = pl.pallas_call(
        clear_kernel,
        out_shape=pltpu.VMEM(user_shape, jnp.float32),
        out_specs=vmem(),
        compiler_params=params(),
        cost_estimate=pl.CostEstimate(flops=10**10, bytes_accessed=0, transcendentals=0),
        name="clear",
    )()
    shards = [items]
    if direct:
        shards += [swap_row(items, k) for k in range(1, half)]
        crossed = swap_row(items, half)
        shards += [crossed] + [swap_row(crossed, k) for k in range(1, half)]
    else:
        shards = [lax.all_gather(items, "row", axis=0, tiled=True)]
    wide = shards[0].shape[0]
    shard_tiles = wide // BLOCK
    edges = [(group[-1] + 1) * shard_tiles for group in groups]

    meta = pl.pallas_call(
        functools.partial(plan_kernel, shard_tiles, keys, edges),
        out_shape=pltpu.SMEM((stages * pad + stages,), jnp.int32),
        in_specs=[smem()] * 3 + [anywhere()],
        out_specs=smem(),
        compiler_params=params(),
        name="plan",
    )(tile_count, tile_rows[0, 0], tile_cols[0, 0], total)

    cost = pl.CostEstimate(
        flops=20 * slots * BLOCK * BLOCK * rank // stages,
        bytes_accessed=(slots // stages) * BLOCK * BLOCK * 4,
        transcendentals=0,
    )
    flipped = []
    for stage, group in enumerate(groups):
        last = stage == stages - 1
        size = len(group)
        panel_shape = (size * wide, rank)
        shapes = [pltpu.VMEM(panel_shape, jnp.bfloat16), pltpu.VMEM(user_shape, jnp.float32)]
        operands = [meta, tiles, words] + [shards[key] for key in group]
        operands += [users, peer_users, total] if stage == 0 else [panel, total]
        if stage == 0:
            shapes.append(pltpu.VMEM(user_shape, jnp.bfloat16))
        if last:
            shapes.append(jax.ShapeDtypeStruct(user_shape, jnp.bfloat16))
        outs = pl.pallas_call(
            functools.partial(user_kernel, stage, stages, size, last),
            out_shape=tuple(shapes),
            in_specs=[smem()] + [vmem()] * (len(operands) - 1),
            out_specs=tuple([vmem()] * len(shapes)),
            input_output_aliases={len(operands) - 1: 1},
            scratch_shapes=[pltpu.VMEM(panel_shape, jnp.bfloat16)],
            compiler_params=params(),
            cost_estimate=cost,
            name="user_terms",
        )(*operands)
        flipped.append(outs[0])
        total = outs[1]
        if stage == 0:
            panel = outs[2]
    terms = outs[-1]
    peer_terms = swap_col(terms)

    sums = [None] * keys
    for parts in ([range(1, stages)] if direct else []) + [range(1)]:
        first = 0 not in parts or not direct
        named = [key for stage in parts for key in groups[stage]]
        shapes = [
            jax.ShapeDtypeStruct(
                (wide, rank), jnp.float32 if key in (0, half) else jnp.bfloat16
            )
            for key in named
        ]
        operands = [meta, tiles, words] + [flipped[stage] for stage in parts]
        if first:
            operands += [terms, peer_terms, panel]
            shapes += [pltpu.VMEM(user_shape, jnp.bfloat16)] * 2
        else:
            operands += [fresh, turned]
        outs = pl.pallas_call(
            functools.partial(item_kernel, tuple(parts), stages, first),
            out_shape=tuple(shapes),
            in_specs=[smem()] + [vmem()] * (len(operands) - 1),
            out_specs=tuple([vmem()] * len(shapes)),
            scratch_shapes=[pltpu.VMEM((len(named) * wide, rank), jnp.float32)],
            compiler_params=params(),
            cost_estimate=cost,
            name="item_terms",
        )(*operands)
        if first:
            fresh, turned = outs[-2:]
        for key, out in zip(named, outs):
            sums[key] = out if key in (0, half) else swap_row(out, key % half)
    users_new = lax.dynamic_slice_in_dim(fresh, col_at * users.shape[0], users.shape[0], 0)

    if direct:
        relay = sums[half]
        for part in sums[half + 1 :]:
            relay = relay + part.astype(jnp.float32)
        parts = sums[:half] + [swap_row(relay.astype(jnp.bfloat16), half)]
        items_new = pl.pallas_call(
            finish_kernel,
            out_shape=jax.ShapeDtypeStruct(items.shape, jnp.bfloat16),
            in_specs=[vmem()] * (1 + len(parts)),
            out_specs=vmem(),
            compiler_params=params(),
            name="finish",
        )(items, *parts)
    else:
        turned_terms = jnp.swapaxes(sums[0].reshape(-1, BLOCK, BLOCK), 1, 2)
        item_grad = lax.psum_scatter(
            turned_terms.reshape(wide, rank), "row", scatter_dimension=0, tiled=True
        )
        values = items.astype(jnp.float32)
        items_new = (values - 0.005 * (item_grad + 0.05 * values)).astype(jnp.bfloat16)
    return (users_new, items_new)


def solution(mesh):
    return jax.shard_map(
        functools.partial(body, mesh.shape["row"], mesh.shape["col"]),
        mesh=mesh,
        in_specs=(
            P(("groups", "row", "col"), None),
            P(("groups", "row", "col"), None),
            P(("groups", "row"), "col", None, None, None),
            P(("groups", "row"), "col", None, None, None),
            P(("groups", "row"), "col", None),
            P(("groups", "row"), "col", None),
            P(("groups", "row"), "col"),
        ),
        out_specs=(P(("groups", "row", "col"), None), P(("groups", "row", "col"), None)),
        check_vma=False,
    )
```

```python
import functools

import jax
import jax.numpy as jnp
from jax import lax
from jax.experimental import pallas as pl
from jax.experimental.pallas import tpu as pltpu
from jax.sharding import PartitionSpec as P

BLOCK = 128
UNROLL = 24
TAIL = 8
FIELD = 8
VMEM_LIMIT = 16 * 1024 * 1024

NN = (((1,), (0,)), ((), ()))

vmem = functools.partial(pl.BlockSpec, memory_space=pltpu.VMEM)
smem = functools.partial(pl.BlockSpec, memory_space=pltpu.SMEM)
anywhere = functools.partial(pl.BlockSpec, memory_space=pl.ANY)


def params(limit=VMEM_LIMIT):
    return pltpu.CompilerParams(vmem_limit_bytes=limit)


def dot(a, b):
    return lax.dot_general(a, b, NN, preferred_element_type=jnp.float32)


def rows_of(index):
    return pl.ds(pl.multiple_of(index * BLOCK, BLOCK), BLOCK)


def tile(index):
    return slice(index * BLOCK, (index + 1) * BLOCK)


def plan_kernel(shard_tiles, keys, edges, region, live, rows, cols, total, meta, found, sem):
    count = live[0, 0]
    slots = cols.shape[1]
    stages = len(edges)
    square = (slots, slots)
    down = lax.broadcasted_iota(jnp.int32, square, 0)
    across = lax.broadcasted_iota(jnp.int32, square, 1)

    v = cols[...]
    if stages > 1:
        v = (v ^ (lax.axis_index("row") * shard_tiles)) & (keys * shard_tiles - 1)
    stage = jnp.zeros_like(v)
    first = jnp.zeros_like(v)
    for i in range(1, stages):
        past = v >= edges[i - 1]
        stage = jnp.where(past, i, stage)
        first = jnp.where(past, edges[i - 1], first)
    word = across[:1] + (rows[...] << FIELD) + ((v - first) << 2 * FIELD)

    def column(row):
        spread = jnp.broadcast_to(row.astype(jnp.float32), square)
        return jnp.sum(jnp.where(down == across, spread, 0.0), axis=1, keepdims=True)

    stage_down = column(stage)
    word_down = column(word)
    stage_across = jnp.broadcast_to(stage.astype(jnp.float32), square)
    ahead = (stage_across == stage_down) & (across < down) & (across < count)
    place = jnp.sum(jnp.where(ahead, 1.0, 0.0), axis=1, keepdims=True)
    place = place + stage_down * region
    here = lax.broadcasted_iota(jnp.int32, (slots, 1), 0) < count
    place = jnp.where(here, place, -1.0)
    wide = (slots, found.shape[1])
    at = lax.broadcasted_iota(jnp.int32, wide, 1).astype(jnp.float32)
    out = jnp.sum(jnp.where(at == place, word_down, 0.0), axis=0, keepdims=True)
    for i in range(stages):
        size = jnp.sum(jnp.where(here & (stage_down == i), 1.0, 0.0), axis=0, keepdims=True)
        out = jnp.where(at[:1] == stages * region + i, size, out)
    found[...] = out.astype(jnp.int32)
    copy = pltpu.make_async_copy(found, meta, sem)
    copy.start()
    copy.wait()


def stage_loop(stage, stages, region, meta, step_of):
    live = meta[0, stages * region + stage]
    mask = (1 << FIELD) - 1

    def group(start, size):
        entries = []
        for j in range(size):
            at = start + j
            word = meta[0, stage * region + at]
            entries.append(
                (word & mask, (word >> FIELD) & mask, word >> 2 * FIELD, at < live)
            )
        step_of(entries)

    def step(i, _):
        group(i * UNROLL, UNROLL)
        return _

    whole = (live + UNROLL - TAIL - 1) // UNROLL
    lax.fori_loop(0, whole, step, 0)

    @pl.when(whole * UNROLL < live)
    def _():
        group(whole * UNROLL, TAIL)


def masked_residual(predicted, tiles, words, slot, live):
    bit = jnp.left_shift(1, lax.broadcasted_iota(jnp.int32, (8, BLOCK), 0))
    bit = jnp.where(live, bit, 0)
    parts = []
    for w in range(BLOCK // 8):
        seen = jnp.broadcast_to(words[slot, pl.ds(w, 1), :], (8, BLOCK)) & bit
        gap = predicted[8 * w : 8 * w + 8] - tiles[slot, pl.ds(8 * w, 8), :].astype(jnp.float32)
        parts.append(jnp.where(seen != 0, gap, 0.0))
    return jnp.concatenate(parts, axis=0).astype(jnp.bfloat16)


def lay_items(shards, panel, flipped):
    per = shards[0].shape[0] // BLOCK
    for s, shard in enumerate(shards):
        for v in range(per):
            block = shard[tile(v)]
            panel[tile(s * per + v)] = block
            flipped[tile(s * per + v)] = block.T


def clear_kernel(total):
    total[...] = jnp.zeros_like(total)


def user_kernel(stage, stages, region, group, last, *refs):
    meta, tiles, words = refs[:3]
    shards = refs[3 : 3 + group]
    if stage == 0:
        mine, theirs = refs[3 + group : 5 + group]
        flipped, total, users = refs[6 + group : 9 + group]
        count = mine.shape[0]
        lead = lax.axis_index("col") == 0
        users[:count] = jnp.where(lead, mine[...], theirs[...])
        users[count:] = jnp.where(lead, theirs[...], mine[...])
    else:
        users = refs[3 + group]
        flipped, total = refs[5 + group : 7 + group]
    panel = refs[-1]
    lay_items(shards, panel, flipped)

    def step_of(entries):
        terms = []
        for slot, u, v, live in entries:
            predicted = dot(users[rows_of(u), :], flipped[rows_of(v), :])
            residual = masked_residual(predicted, tiles, words, slot, live)
            terms.append(dot(residual, panel[rows_of(v), :]))
        for (slot, u, v, live), term in zip(entries, terms):
            total[rows_of(u), :] += term

    stage_loop(stage, stages, region, meta, step_of)
    if last:
        refs[-2][...] = total[...].astype(jnp.bfloat16)


def item_kernel(parts, stages, region, first, *refs):
    meta, tiles, words = refs[:3]
    flips = refs[3 : 3 + len(parts)]
    refs = refs[3 + len(parts) :]
    total = refs[-1]
    if first:
        mine, theirs, users = refs[:3]
        outs = refs[3:-3]
        fresh, turned = refs[-3:-1]
        for u in range(users.shape[0] // BLOCK):
            values = users[tile(u)].astype(jnp.float32)
            gradient = mine[tile(u)].astype(jnp.float32) + theirs[tile(u)].astype(jnp.float32)
            new = (values - 0.02 * (gradient + 0.05 * values)).astype(jnp.bfloat16)
            fresh[tile(u)] = new
            turned[tile(u)] = new.T
    else:
        fresh, turned = refs[:2]
        outs = refs[2:-1]
    total[...] = jnp.zeros_like(total)
    base = 0
    for stage, flipped in zip(parts, flips):

        def step_of(entries, base=base, flipped=flipped):
            terms = []
            for slot, u, v, live in entries:
                predicted = dot(fresh[rows_of(u), :], flipped[rows_of(v), :])
                residual = masked_residual(predicted, tiles, words, slot, live)
                terms.append(dot(turned[rows_of(u), :], residual))
            for (slot, u, v, live), term in zip(entries, terms):
                total[rows_of(v + base), :] += term

        stage_loop(stage, stages, region, meta, step_of)
        base += flipped.shape[0] // BLOCK
    size = outs[0].shape[0]
    for s, out in enumerate(outs):
        out[...] = total[s * size : (s + 1) * size].astype(out.dtype)


def finish_kernel(items, *refs):
    out = refs[-1]
    for v in range(items.shape[0] // BLOCK):
        gradient = refs[0][tile(v)].astype(jnp.float32)
        for part in refs[1:-1]:
            gradient = gradient + part[tile(v)].astype(jnp.float32)
        values = items[tile(v)].astype(jnp.float32)
        out[tile(v)] = (values - 0.005 * (gradient.T + 0.05 * values)).astype(jnp.bfloat16)


def body(n_row, n_col, users, items, ratings, observed, tile_rows, tile_cols, tile_count):
    tiles = ratings[0, 0]
    words = observed[0, 0]
    slots = tiles.shape[0]
    rank = users.shape[-1]
    pad = slots + UNROLL
    per = items.shape[0] // BLOCK
    direct = items.shape[0] == per * BLOCK and n_row > 2
    direct = direct and (n_row & (n_row - 1)) == 0 and (per & (per - 1)) == 0
    keys = n_row if direct else 1
    half = n_row // 2
    groups = [[0]]
    if direct:
        groups = [range(half + 1), range(half + 1, n_row - 1), range(n_row - 1, n_row)]
        groups = [list(group) for group in groups if len(group)]
    stages = len(groups)
    col_at = lax.axis_index("col")

    def swap_row(x, k):
        return lax.ppermute(x, "row", [(i, i ^ k) for i in range(n_row)])

    def swap_col(x):
        return lax.ppermute(x, "col", [(i, i ^ 1) for i in range(n_col)])

    peer_users = swap_col(users)
    user_shape = (n_col * users.shape[0], rank)
    total = pl.pallas_call(
        clear_kernel,
        out_shape=pltpu.VMEM(user_shape, jnp.float32),
        out_specs=vmem(),
        compiler_params=params(),
        cost_estimate=pl.CostEstimate(flops=10**10, bytes_accessed=0, transcendentals=0),
        name="clear",
    )()
    shards = [items]
    if direct:
        shards += [swap_row(items, k) for k in range(1, half)]
        crossed = swap_row(items, half)
        shards += [crossed] + [swap_row(crossed, k) for k in range(1, half)]
    else:
        shards = [lax.all_gather(items, "row", axis=0, tiled=True)]
    wide = shards[0].shape[0]
    shard_tiles = wide // BLOCK
    edges = [(group[-1] + 1) * shard_tiles for group in groups]

    words_out = -(-(stages * pad + stages) // BLOCK) * BLOCK
    meta = pl.pallas_call(
        functools.partial(plan_kernel, shard_tiles, keys, edges, pad),
        out_shape=pltpu.SMEM((1, words_out), jnp.int32),
        in_specs=[smem(), vmem(), vmem(), anywhere()],
        out_specs=smem(),
        scratch_shapes=[pltpu.VMEM((1, words_out), jnp.int32), pltpu.SemaphoreType.DMA],
        compiler_params=params(),
        name="plan",
    )(tile_count, tile_rows[0], tile_cols[0], total)

    cost = pl.CostEstimate(
        flops=slots * BLOCK * BLOCK,
        bytes_accessed=0,
        transcendentals=0,
    )
    flipped = []
    for stage, group in enumerate(groups):
        last = stage == stages - 1
        size = len(group)
        panel_shape = (size * wide, rank)
        shapes = [pltpu.VMEM(panel_shape, jnp.bfloat16), pltpu.VMEM(user_shape, jnp.float32)]
        operands = [meta, tiles, words] + [shards[key] for key in group]
        operands += [users, peer_users, total] if stage == 0 else [panel, total]
        if stage == 0:
            shapes.append(pltpu.VMEM(user_shape, jnp.bfloat16))
        if last:
            shapes.append(jax.ShapeDtypeStruct(user_shape, jnp.bfloat16))
        outs = pl.pallas_call(
            functools.partial(user_kernel, stage, stages, pad, size, last),
            out_shape=tuple(shapes),
            in_specs=[smem()] + [vmem()] * (len(operands) - 1),
            out_specs=tuple([vmem()] * len(shapes)),
            input_output_aliases={len(operands) - 1: 1},
            scratch_shapes=[pltpu.VMEM(panel_shape, jnp.bfloat16)],
            compiler_params=params(),
            cost_estimate=cost,
            name="user_terms",
        )(*operands)
        flipped.append(outs[0])
        total = outs[1]
        if stage == 0:
            panel = outs[2]
    terms = outs[-1]
    peer_terms = swap_col(terms)

    sums = [None] * keys
    for parts in ([range(1, stages)] if direct else []) + [range(1)]:
        first = 0 not in parts or not direct
        named = [key for stage in parts for key in groups[stage]]
        shapes = [
            jax.ShapeDtypeStruct(
                (wide, rank), jnp.float32 if key in (0, half) else jnp.bfloat16
            )
            for key in named
        ]
        operands = [meta, tiles, words] + [flipped[stage] for stage in parts]
        if first:
            operands += [terms, peer_terms, panel]
            shapes += [pltpu.VMEM(user_shape, jnp.bfloat16)] * 2
        else:
            operands += [fresh, turned]
        outs = pl.pallas_call(
            functools.partial(item_kernel, tuple(parts), stages, pad, first),
            out_shape=tuple(shapes),
            in_specs=[smem()] + [vmem()] * (len(operands) - 1),
            out_specs=tuple([vmem()] * len(shapes)),
            scratch_shapes=[pltpu.VMEM((len(named) * wide, rank), jnp.float32)],
            compiler_params=params(),
            cost_estimate=cost,
            name="item_terms",
        )(*operands)
        if first:
            fresh, turned = outs[-2:]
        for key, out in zip(named, outs):
            sums[key] = out if key in (0, half) else swap_row(out, key % half)
    users_new = lax.dynamic_slice_in_dim(fresh, col_at * users.shape[0], users.shape[0], 0)

    if direct:
        relay = sums[half]
        for part in sums[half + 1 :]:
            relay = relay + part.astype(jnp.float32)
        parts = sums[:half] + [swap_row(relay.astype(jnp.bfloat16), half)]
        items_new = pl.pallas_call(
            finish_kernel,
            out_shape=jax.ShapeDtypeStruct(items.shape, jnp.bfloat16),
            in_specs=[vmem()] * (1 + len(parts)),
            out_specs=vmem(),
            compiler_params=params(),
            name="finish",
        )(items, *parts)
    else:
        turned_terms = jnp.swapaxes(sums[0].reshape(-1, BLOCK, BLOCK), 1, 2)
        item_grad = lax.psum_scatter(
            turned_terms.reshape(wide, rank), "row", scatter_dimension=0, tiled=True
        )
        values = items.astype(jnp.float32)
        items_new = (values - 0.005 * (item_grad + 0.05 * values)).astype(jnp.bfloat16)
    return (users_new, items_new)


def solution(mesh):
    return jax.shard_map(
        functools.partial(body, mesh.shape["row"], mesh.shape["col"]),
        mesh=mesh,
        in_specs=(
            P(("groups", "row", "col"), None),
            P(("groups", "row", "col"), None),
            P(("groups", "row"), "col", None, None, None),
            P(("groups", "row"), "col", None, None, None),
            P(("groups", "row"), "col", None),
            P(("groups", "row"), "col", None),
            P(("groups", "row"), "col"),
        ),
        out_specs=(P(("groups", "row", "col"), None), P(("groups", "row", "col"), None)),
        check_vma=False,
    )
```

```python
import functools

import jax
import jax.numpy as jnp
from jax import lax
from jax.experimental import pallas as pl
from jax.experimental.pallas import tpu as pltpu
from jax.sharding import PartitionSpec as P

BLOCK = 128
UNROLL = 24
TAILS = (8, 16)
FIELD = 10
PLAN_UNROLL = 8
VMEM_LIMIT = 16 * 1024 * 1024

NN = (((1,), (0,)), ((), ()))

vmem = functools.partial(pl.BlockSpec, memory_space=pltpu.VMEM)
smem = functools.partial(pl.BlockSpec, memory_space=pltpu.SMEM)
anywhere = functools.partial(pl.BlockSpec, memory_space=pl.ANY)


def params(limit=VMEM_LIMIT):
    return pltpu.CompilerParams(vmem_limit_bytes=limit)


def dot(a, b):
    return lax.dot_general(a, b, NN, preferred_element_type=jnp.float32)


def rows_of(index):
    return pl.ds(pl.multiple_of(index * BLOCK, BLOCK), BLOCK)


def tile(index):
    return slice(index * BLOCK, (index + 1) * BLOCK)


def plan_kernel(shard_tiles, keys, edges, live, rows, cols, total, meta):
    count = live[0, 0]
    me = lax.axis_index("row")
    stages = len(edges)
    region = (meta.shape[0] - stages) // stages

    def put(i, places):
        places = list(places)
        packed = []
        for j in range(PLAN_UNROLL):
            t = i * PLAN_UNROLL + j
            at = jnp.minimum(t, rows.shape[0] - 1)
            v = cols[at]
            if stages > 1:
                v = (v ^ (me * shard_tiles)) & (keys * shard_tiles - 1)
            packed.append((t, v, at + (rows[at] << FIELD)))
        for t, v, word in packed:
            spot, base = places[0], jnp.int32(0)
            inside = [v < edges[0]]
            for stage in range(1, stages):
                past = v >= edges[stage - 1]
                spot = jnp.where(past, stage * region + places[stage], spot)
                base = jnp.where(past, edges[stage - 1], base)
                inside.append(past & (v < edges[stage]))
            meta[spot] = word + ((v - base) << 2 * FIELD)
            for stage in range(stages):
                places[stage] += jnp.where(inside[stage] & (t < count), 1, 0)
        return tuple(places)

    trips = (count + PLAN_UNROLL - 1) // PLAN_UNROLL
    places = lax.fori_loop(0, trips, put, (jnp.int32(0),) * stages)
    for stage in range(stages):
        for at in range(UNROLL):
            meta[stage * region + places[stage] + at] = 0
        meta[stages * region + stage] = places[stage]


def stage_loop(stage, stages, meta, step_of):
    region = (meta.shape[0] - stages) // stages
    live = meta[stages * region + stage]
    mask = (1 << FIELD) - 1

    def group(start, size):
        entries = []
        for j in range(size):
            at = start + j
            word = meta[stage * region + at]
            entries.append(
                (word & mask, (word >> FIELD) & mask, word >> 2 * FIELD, at < live)
            )
        step_of(entries)

    def step(i, _):
        group(i * UNROLL, UNROLL)
        return _

    whole = (live + UNROLL - TAILS[-1] - 1) // UNROLL
    lax.fori_loop(0, whole, step, 0)
    rest = live - whole * UNROLL
    for less, size in zip((0,) + TAILS, TAILS):

        @pl.when((rest > less) & (rest <= size))
        def _(size=size):
            group(whole * UNROLL, size)


def masked_residual(predicted, tiles, words, slot, live):
    bit = jnp.left_shift(1, lax.broadcasted_iota(jnp.int32, (8, BLOCK), 0))
    bit = jnp.where(live, bit, 0)
    parts = []
    for w in range(BLOCK // 8):
        seen = jnp.broadcast_to(words[slot, pl.ds(w, 1), :], (8, BLOCK)) & bit
        gap = predicted[8 * w : 8 * w + 8] - tiles[slot, pl.ds(8 * w, 8), :].astype(jnp.float32)
        parts.append(jnp.where(seen != 0, gap, 0.0))
    return jnp.concatenate(parts, axis=0).astype(jnp.bfloat16)


def lay_items(shards, panel, flipped):
    per = shards[0].shape[0] // BLOCK
    for s, shard in enumerate(shards):
        for v in range(per):
            block = shard[tile(v)]
            panel[tile(s * per + v)] = block
            flipped[tile(s * per + v)] = block.T


def clear_kernel(total):
    total[...] = jnp.zeros_like(total)


def user_kernel(stage, stages, group, last, *refs):
    meta, tiles, words = refs[:3]
    shards = refs[3 : 3 + group]
    if stage == 0:
        mine, theirs = refs[3 + group : 5 + group]
        flipped, total, users = refs[6 + group : 9 + group]
        count = mine.shape[0]
        lead = lax.axis_index("col") == 0
        users[:count] = jnp.where(lead, mine[...], theirs[...])
        users[count:] = jnp.where(lead, theirs[...], mine[...])
    else:
        users = refs[3 + group]
        flipped, total = refs[5 + group : 7 + group]
    panel = refs[-1]
    lay_items(shards, panel, flipped)

    def step_of(entries):
        terms = []
        for slot, u, v, live in entries:
            predicted = dot(users[rows_of(u), :], flipped[rows_of(v), :])
            residual = masked_residual(predicted, tiles, words, slot, live)
            terms.append(dot(residual, panel[rows_of(v), :]))
        for (slot, u, v, live), term in zip(entries, terms):
            total[rows_of(u), :] += term

    stage_loop(stage, stages, meta, step_of)
    if last:
        refs[-2][...] = total[...].astype(jnp.bfloat16)


def item_kernel(parts, stages, first, *refs):
    meta, tiles, words = refs[:3]
    flips = refs[3 : 3 + len(parts)]
    refs = refs[3 + len(parts) :]
    total = refs[-1]
    if first:
        mine, theirs, users = refs[:3]
        outs = refs[3:-3]
        fresh, turned = refs[-3:-1]
        for u in range(users.shape[0] // BLOCK):
            values = users[tile(u)].astype(jnp.float32)
            gradient = mine[tile(u)].astype(jnp.float32) + theirs[tile(u)].astype(jnp.float32)
            new = (values - 0.02 * (gradient + 0.05 * values)).astype(jnp.bfloat16)
            fresh[tile(u)] = new
            turned[tile(u)] = new.T
    else:
        fresh, turned = refs[:2]
        outs = refs[2:-1]
    total[...] = jnp.zeros_like(total)
    base = 0
    for stage, flipped in zip(parts, flips):

        def step_of(entries, base=base, flipped=flipped):
            terms = []
            for slot, u, v, live in entries:
                predicted = dot(fresh[rows_of(u), :], flipped[rows_of(v), :])
                residual = masked_residual(predicted, tiles, words, slot, live)
                terms.append(dot(turned[rows_of(u), :], residual))
            for (slot, u, v, live), term in zip(entries, terms):
                total[rows_of(v + base), :] += term

        stage_loop(stage, stages, meta, step_of)
        base += flipped.shape[0] // BLOCK
    size = outs[0].shape[0]
    for s, out in enumerate(outs):
        out[...] = total[s * size : (s + 1) * size].astype(out.dtype)


def finish_kernel(items, *refs):
    out = refs[-1]
    for v in range(items.shape[0] // BLOCK):
        gradient = refs[0][tile(v)].astype(jnp.float32)
        for part in refs[1:-1]:
            gradient = gradient + part[tile(v)].astype(jnp.float32)
        values = items[tile(v)].astype(jnp.float32)
        out[tile(v)] = (values - 0.005 * (gradient.T + 0.05 * values)).astype(jnp.bfloat16)


def body(n_row, n_col, users, items, ratings, observed, tile_rows, tile_cols, tile_count):
    tiles = ratings[0, 0]
    words = observed[0, 0]
    slots = tiles.shape[0]
    rank = users.shape[-1]
    pad = slots + UNROLL
    per = items.shape[0] // BLOCK
    direct = items.shape[0] == per * BLOCK and n_row > 2
    direct = direct and (n_row & (n_row - 1)) == 0 and (per & (per - 1)) == 0
    keys = n_row if direct else 1
    half = n_row // 2
    groups = [[0]]
    if direct:
        groups = [range(half + 1), range(half + 1, n_row - 1), range(n_row - 1, n_row)]
        groups = [list(group) for group in groups if len(group)]
    stages = len(groups)
    col_at = lax.axis_index("col")

    def swap_row(x, k):
        return lax.ppermute(x, "row", [(i, i ^ k) for i in range(n_row)])

    def swap_col(x):
        return lax.ppermute(x, "col", [(i, i ^ 1) for i in range(n_col)])

    peer_users = swap_col(users)
    user_shape = (n_col * users.shape[0], rank)
    total = pl.pallas_call(
        clear_kernel,
        out_shape=pltpu.VMEM(user_shape, jnp.float32),
        out_specs=vmem(),
        compiler_params=params(),
        cost_estimate=pl.CostEstimate(flops=10**10, bytes_accessed=0, transcendentals=0),
        name="clear",
    )()
    shards = [items]
    if direct:
        shards += [swap_row(items, k) for k in range(1, half)]
        crossed = swap_row(items, half)
        shards += [crossed] + [swap_row(crossed, k) for k in range(1, half)]
    else:
        shards = [lax.all_gather(items, "row", axis=0, tiled=True)]
    wide = shards[0].shape[0]
    shard_tiles = wide // BLOCK
    edges = [(group[-1] + 1) * shard_tiles for group in groups]

    meta = pl.pallas_call(
        functools.partial(plan_kernel, shard_tiles, keys, edges),
        out_shape=pltpu.SMEM((stages * pad + stages,), jnp.int32),
        in_specs=[smem()] * 3 + [anywhere()],
        out_specs=smem(),
        compiler_params=params(),
        name="plan",
    )(tile_count, tile_rows[0, 0], tile_cols[0, 0], total)

    cost = pl.CostEstimate(
        flops=20 * slots * BLOCK * BLOCK * rank // stages,
        bytes_accessed=(slots // stages) * BLOCK * BLOCK * 4,
        transcendentals=0,
    )
    flipped = []
    for stage, group in enumerate(groups):
        last = stage == stages - 1
        size = len(group)
        panel_shape = (size * wide, rank)
        shapes = [pltpu.VMEM(panel_shape, jnp.bfloat16), pltpu.VMEM(user_shape, jnp.float32)]
        operands = [meta, tiles, words] + [shards[key] for key in group]
        operands += [users, peer_users, total] if stage == 0 else [panel, total]
        if stage == 0:
            shapes.append(pltpu.VMEM(user_shape, jnp.bfloat16))
        if last:
            shapes.append(jax.ShapeDtypeStruct(user_shape, jnp.bfloat16))
        outs = pl.pallas_call(
            functools.partial(user_kernel, stage, stages, size, last),
            out_shape=tuple(shapes),
            in_specs=[smem()] + [vmem()] * (len(operands) - 1),
            out_specs=tuple([vmem()] * len(shapes)),
            input_output_aliases={len(operands) - 1: 1},
            scratch_shapes=[pltpu.VMEM(panel_shape, jnp.bfloat16)],
            compiler_params=params(),
            cost_estimate=cost,
            name="user_terms",
        )(*operands)
        flipped.append(outs[0])
        total = outs[1]
        if stage == 0:
            panel = outs[2]
    terms = outs[-1]
    peer_terms = swap_col(terms)

    sums = [None] * keys
    for parts in ([range(1, stages)] if direct else []) + [range(1)]:
        first = 0 not in parts or not direct
        named = [key for stage in parts for key in groups[stage]]
        shapes = [
            jax.ShapeDtypeStruct(
                (wide, rank), jnp.float32 if key in (0, half) else jnp.bfloat16
            )
            for key in named
        ]
        operands = [meta, tiles, words] + [flipped[stage] for stage in parts]
        if first:
            operands += [terms, peer_terms, panel]
            shapes += [pltpu.VMEM(user_shape, jnp.bfloat16)] * 2
        else:
            operands += [fresh, turned]
        outs = pl.pallas_call(
            functools.partial(item_kernel, tuple(parts), stages, first),
            out_shape=tuple(shapes),
            in_specs=[smem()] + [vmem()] * (len(operands) - 1),
            out_specs=tuple([vmem()] * len(shapes)),
            scratch_shapes=[pltpu.VMEM((len(named) * wide, rank), jnp.float32)],
            compiler_params=params(),
            cost_estimate=cost,
            name="item_terms",
        )(*operands)
        if first:
            fresh, turned = outs[-2:]
        for key, out in zip(named, outs):
            sums[key] = out if key in (0, half) else swap_row(out, key % half)
    users_new = lax.dynamic_slice_in_dim(fresh, col_at * users.shape[0], users.shape[0], 0)

    if direct:
        relay = sums[half]
        for part in sums[half + 1 :]:
            relay = relay + part.astype(jnp.float32)
        parts = sums[:half] + [swap_row(relay.astype(jnp.bfloat16), half)]
        items_new = pl.pallas_call(
            finish_kernel,
            out_shape=jax.ShapeDtypeStruct(items.shape, jnp.bfloat16),
            in_specs=[vmem()] * (1 + len(parts)),
            out_specs=vmem(),
            compiler_params=params(),
            name="finish",
        )(items, *parts)
    else:
        turned_terms = jnp.swapaxes(sums[0].reshape(-1, BLOCK, BLOCK), 1, 2)
        item_grad = lax.psum_scatter(
            turned_terms.reshape(wide, rank), "row", scatter_dimension=0, tiled=True
        )
        values = items.astype(jnp.float32)
        items_new = (values - 0.005 * (item_grad + 0.05 * values)).astype(jnp.bfloat16)
    return (users_new, items_new)


def solution(mesh):
    return jax.shard_map(
        functools.partial(body, mesh.shape["row"], mesh.shape["col"]),
        mesh=mesh,
        in_specs=(
            P(("groups", "row", "col"), None),
            P(("groups", "row", "col"), None),
            P(("groups", "row"), "col", None, None, None),
            P(("groups", "row"), "col", None, None, None),
            P(("groups", "row"), "col", None),
            P(("groups", "row"), "col", None),
            P(("groups", "row"), "col"),
        ),
        out_specs=(P(("groups", "row", "col"), None), P(("groups", "row", "col"), None)),
        check_vma=False,
    )
```
